256 devices in a mesh: store: 16 (over z_lo, x), group: 16 (over y, z_hi, core).
Axes of the slice: x: 4, y: 4, z: 8 (z_hi: 2, z_lo: 4; z = z_hi * 4 + z_lo), core: 2. Of those that a mesh axis runs over, the one named last changes fastest.
Arguments:
- activations: bfloat16 [1024, 16, 64, 256], P('group', 'store'), may hold values from -6 to 6
- out_grads: bfloat16 [1024, 16, 64, 256], P('group', 'store'), may hold values from -6 to 6
- stored: bfloat16 [12288, 16, 4096], P('group', 'store'), may hold values from -0.0019989014 to 0.0019989014
- lengths: int32 [1024], P('group'), may hold values from 64 to 256, as said below
- store_ids: int32 [12288], P('group'), may hold values from 0 to 767, as said below
Outputs:
- scores: float32 [1024, 12288], P('store', 'group')
The draws below stay inside these ranges and needn't reach their ends.
Inputs may be any that keep to these rules, and one draw needn't show every extreme that they name: `lengths`: one query pair has all 256 slots live. `store_ids`: each aligned block of 768 entries is a permutation of 0 to 767.
All inputs are finite; a program needn't handle non-finite values.
Results may differ from the reference program's by a relative error of at most 0.0029.
Values may be sent and summed in bfloat16 or wider, within the bound.
No kernel may reach another device: no remote copies, remote signals or barrier semaphores. Data moves between devices by JAX's collectives and lax.ppermute only.
A program may use at most 64 MiB of HBM per device.

```python
import jax
import jax.numpy as jnp

K = 64
L = 16
TOK = 256
S_DEV = 768
QP = 1024
S = 12288


def draw_lengths(key, part):
    key = jax.random.fold_in(key, 11)
    values = jax.random.randint(key, (QP,), TOK // 4, TOK + 1, dtype=jnp.int32)
    return values.at[0].set(TOK)


def draw_store_ids(key, part):
    key = jax.random.fold_in(key, 23)
    subkeys = jax.random.split(key, S // S_DEV)
    perms = jax.vmap(lambda one_key: jax.random.permutation(one_key, S_DEV))(subkeys)
    return perms.reshape(S).astype(jnp.int32)


def level_of(rng, dims, shards, low, top_value):
    gain, own = 1.0, jax.random.fold_in(rng, 6)
    for axis_at, blocks in shards:
        steps = jnp.exp(jax.random.uniform(jax.random.fold_in(own, axis_at), (blocks,), jnp.float32, low / len(shards), top_value / len(shards)))
        gain = gain * jnp.repeat(steps, dims[axis_at] // blocks).reshape([-1 if axis == axis_at else 1 for axis in range(len(dims))])
    return gain


def gaussian(rng, dims, width, limit, cuts=(), kind=jnp.bfloat16):
    drawn = width * jax.random.normal(rng, dims, jnp.float32)
    if cuts:
        drawn = drawn * level_of(rng, dims, cuts, -0.22, 0.18)
    return jnp.clip(drawn, -limit, limit).astype(kind)


def setup_inputs(seed: int = 0) -> dict:
    keys = jax.random.split(jax.random.key(seed), 6)
    activations = gaussian(keys[0], (QP, L, K, TOK), 1.0, 6.0, ((0, 16), (1, 16)))
    out_grads = gaussian(keys[1], (QP, L, K, TOK), 1.0, 6.0, ((0, 16), (1, 16)))
    stored = gaussian(keys[2], (S, L, K * K), 0.0003, 0.0019989014, ((0, 16), (1, 16)))
    lengths = draw_lengths(jax.random.fold_in(keys[5], 71), 0)
    store_ids = draw_store_ids(jax.random.fold_in(keys[5], 71), 0)
    return {"activations": activations, "out_grads": out_grads, "stored": stored, "lengths": lengths, "store_ids": store_ids}


def reference(activations, out_grads, stored, lengths, store_ids):
    slots = jnp.arange(TOK, dtype=jnp.int32)
    live = slots[None, :] < lengths[:, None]
    layer_grads = []
    for layer in range(L):
        acts = jnp.where(live[:, None, :], activations[:, layer], jnp.zeros((), activations.dtype))
        prod = jnp.einsum("pit,pjt->pij", out_grads[:, layer].astype(jnp.float32), acts.astype(jnp.float32))
        layer_grads.append(prod.astype(jnp.bfloat16).reshape(QP, K * K))
    query_grad = jnp.stack(layer_grads, axis=1).reshape(QP, L * K * K)
    raw = jnp.dot(query_grad, stored.reshape(S, L * K * K).T, preferred_element_type=jnp.float32)
    blocks = jnp.arange(S, dtype=jnp.int32) // S_DEV
    columns = (blocks * S_DEV + store_ids).astype(jnp.int32)
    return jnp.take(raw, columns, axis=1)
```

```python
import functools

import jax
import jax.numpy as jnp
from jax import lax
from jax.experimental import pallas as pl
from jax.experimental.pallas import tpu as pltpu
from jax.sharding import PartitionSpec as P

CHUNKS = 2
PAIRS = 64
ROWS = PAIRS // CHUNKS
WIDTH = 64
SLOTS = 256
FEATURES = WIDTH * WIDTH
HELD = 768
STEP_PAIRS = 8
PITCH = 72
COLS = 256
F32 = jnp.float32
BF16 = jnp.bfloat16


def node(x, z_lo, y, z_hi, core):
    return (z_lo % 4) * 4 + x % 4, ((y % 4) * 2 + z_hi % 2) * 2 + core % 2


def group_pairs(move):
    pairs = []
    for y in range(4):
        for z_hi in range(2):
            for core in range(2):
                dst = move(y, z_hi, core)
                if dst is not None:
                    pairs.append((node(0, 0, y, z_hi, core)[1], node(0, 0, *dst)[1]))
    return pairs


def place():
    store, group = lax.axis_index("store"), lax.axis_index("group")
    return store % 4, store // 4, group // 4, (group // 2) % 2, group % 2


def grad_kernel(chunk, *refs):
    lengths_hbm, acts_hbm, grads_hbm, *earlier = refs[: 3 + chunk]
    out_ref, *whole = refs[3 + chunk : -5]
    acts_ref, grads_ref, lengths_ref, wide_ref, sems = refs[-5:]
    first = chunk * ROWS

    def copies(n):
        src, dst = pl.ds(first + n * STEP_PAIRS, STEP_PAIRS), pl.ds(n * STEP_PAIRS, STEP_PAIRS)
        return (
            pltpu.make_async_copy(acts_hbm.at[src, 0], acts_ref.at[dst], sems.at[2 * n]),
            pltpu.make_async_copy(grads_hbm.at[src, 0], grads_ref.at[dst], sems.at[2 * n + 1]),
        )

    steps = ROWS // STEP_PAIRS
    lengths_copy = pltpu.make_async_copy(lengths_hbm, lengths_ref, sems.at[2 * steps])
    lengths_copy.start()
    for n in range(steps):
        for copy in copies(n):
            copy.start()
    lengths_copy.wait()
    slot = lax.broadcasted_iota(jnp.int32, (WIDTH, SLOTS), 1)
    for n in range(steps):
        for copy in copies(n):
            copy.wait()
        for p in range(n * STEP_PAIRS, (n + 1) * STEP_PAIRS):
            acts = acts_ref[p]
            acts = jnp.where(slot < lengths_ref[first + p], acts, jnp.zeros_like(acts))
            wide_ref[pl.ds(p * PITCH, WIDTH), :] = lax.dot_general(
                grads_ref[p],
                jnp.concatenate([acts, acts], axis=0),
                (((1,), (1,)), ((), ())),
                preferred_element_type=F32,
            )
    low = lax.broadcasted_iota(jnp.int32, (ROWS, 128), 1) < WIDTH
    for c in range(FEATURES // 128):
        even = wide_ref[pl.ds(2 * c, ROWS, stride=PITCH), :]
        odd = wide_ref[pl.ds(2 * c + 1, ROWS, stride=PITCH), :]
        out_ref[:, c * 128 : (c + 1) * 128] = jnp.where(low, even, odd).astype(BF16)
    for whole_ref in whole:
        for n, piece in enumerate((*earlier, out_ref)):
            whole_ref[n * ROWS : (n + 1) * ROWS, :] = piece[...]


def query_grads(lengths, activations, out_grads, earlier):
    chunk = len(earlier)
    last = chunk == CHUNKS - 1
    hbm = pl.BlockSpec(memory_space=pltpu.HBM)
    return pl.pallas_call(
        functools.partial(grad_kernel, chunk),
        out_shape=[jax.ShapeDtypeStruct((ROWS, FEATURES), BF16)]
        + [jax.ShapeDtypeStruct((PAIRS, FEATURES), BF16)] * last,
        in_specs=[hbm] * 3 + [pl.BlockSpec(memory_space=pltpu.VMEM)] * chunk,
        scratch_shapes=[
            pltpu.VMEM((ROWS, WIDTH, SLOTS), BF16),
            pltpu.VMEM((ROWS, WIDTH, SLOTS), BF16),
            pltpu.SMEM((PAIRS,), jnp.int32),
            pltpu.VMEM((ROWS * PITCH, 128), F32),
            pltpu.SemaphoreType.DMA((2 * (ROWS // STEP_PAIRS) + 1,)),
        ],
        compiler_params=pltpu.CompilerParams(vmem_limit_bytes=16 << 20),
        cost_estimate=pl.CostEstimate(
            flops=chunk * 8 * FEATURES * SLOTS * PAIRS * ROWS, bytes_accessed=0, transcendentals=0
        ),
        name="query_grads",
    )(lengths, activations, out_grads, *earlier)


def score_kernel(own_ref, *refs):
    blocks, (mine_ref, other_ref), outs = refs[:4], refs[4:6], refs[6:]
    step = pl.program_id(0)
    x, _, y, z_hi, core = place()

    def part(weights_ref, rel_core, tile):
        got = lax.dot_general(
            jnp.concatenate(
                [own_ref[...].reshape(4 * ROWS, FEATURES)] + [b[...] for b in blocks], axis=0
            ),
            weights_ref[...],
            (((1,), (1,)), ((), ())),
            preferred_element_type=F32,
        ).astype(BF16)
        for rel_z in range(2):
            to_x = 2 * ((z_hi + rel_z) % 2) + core
            away = (to_x - x + 4) % 4
            if rel_core == 0:
                buf = jnp.where(away == 0, 3, jnp.where(away == 1, 1, jnp.where(away == 2, 0, 2)))
            else:
                buf = jnp.where(away == 0, 2, jnp.where(away == 1, 0, jnp.where(away == 2, 1, 3)))
            for b in range(4):

                @pl.when(buf == b)
                def _():
                    cols = slice(tile * COLS, (tile + 1) * COLS)
                    if rel_z == 0:
                        outs[b][:, cols] = got[: 4 * ROWS]
                    else:
                        for j, dy in enumerate((0, 3, 1, 2)):
                            row = pl.multiple_of(((y + dy) % 4) * ROWS, ROWS)
                            at = (4 + j) * ROWS
                            outs[b][pl.ds(row, ROWS), cols] = got[at : at + ROWS]

    tiles = HELD // COLS
    for s in range(2 * tiles):

        @pl.when(step == s)
        def _():
            part(mine_ref if s < tiles else other_ref, s // tiles, s % tiles)


def partial_scores(own, fars, mine, other, chunk):
    tiles = HELD // COLS
    whole = pl.BlockSpec((ROWS, FEATURES), lambda i: (0, 0))
    out = pl.BlockSpec((4 * ROWS, HELD), lambda i: (0, 0))
    return pl.pallas_call(
        score_kernel,
        out_shape=[jax.ShapeDtypeStruct((4 * ROWS, HELD), BF16)] * 4,
        grid=(2 * tiles,),
        in_specs=[pl.BlockSpec((4, ROWS, FEATURES), lambda i: (0, chunk, 0))]
        + [whole] * 4
        + [
            pl.BlockSpec((COLS, FEATURES), lambda i: (jnp.minimum(i, tiles - 1), 0)),
            pl.BlockSpec((COLS, FEATURES), lambda i: (jnp.maximum(i - tiles, 0), 0)),
        ],
        out_specs=[out] * 4,
        compiler_params=pltpu.CompilerParams(vmem_limit_bytes=24 << 20),
        cost_estimate=pl.CostEstimate(
            flops=2 * 8 * ROWS * FEATURES * 2 * HELD,
            bytes_accessed=2 * FEATURES * (2 * HELD + 8 * ROWS),
            transcendentals=0,
        ),
        name="partial_scores",
    )(own, *fars, mine, other)


def cross_sum_kernel(a_ref, b_ref, c_ref, d_ref, own_ref, keep_ref, *outs):
    x, z_lo, _, _, core = place()
    match = (x % 2) == core
    for k in range(4):
        rows = pl.ds(pl.multiple_of(((z_lo + k) % 4) * ROWS, ROWS), ROWS)
        last = jnp.where(match, own_ref[rows, :].astype(F32), d_ref[rows, :].astype(F32))
        total = a_ref[rows, :].astype(F32) + b_ref[rows, :].astype(F32)
        total = total + (c_ref[rows, :].astype(F32) + last)
        if k == 0:
            keep_ref[...] = total
        else:
            outs[k - 1][...] = total.astype(BF16)


def cross_sum(*parts):
    return pl.pallas_call(
        cross_sum_kernel,
        out_shape=[jax.ShapeDtypeStruct((ROWS, HELD), F32)]
        + [jax.ShapeDtypeStruct((ROWS, HELD), BF16)] * 3,
        compiler_params=pltpu.CompilerParams(vmem_limit_bytes=16 << 20),
        name="cross_sum",
    )(*parts)


def final_kernel(*refs):
    pick_ref, out_ref = refs[-2:]
    totals = []
    for n in range(CHUNKS):
        keep, first, second, third = refs[4 * n : 4 * n + 4]
        total = keep[...] + first[...].astype(F32)
        totals.append(total + (second[...].astype(F32) + third[...].astype(F32)))
    total = jnp.concatenate(totals, axis=0)
    high = total.astype(BF16)
    rest = total - high.astype(F32)
    middle = rest.astype(BF16)
    low = (rest - middle.astype(F32)).astype(BF16)
    picked = lax.dot_general(
        jnp.concatenate([high, middle, low], axis=0),
        pick_ref[...],
        (((1,), (0,)), ((), ())),
        preferred_element_type=F32,
    )
    out_ref[...] = picked[:PAIRS] + (picked[PAIRS : 2 * PAIRS] + picked[2 * PAIRS :])


def final_sum(parts, pick):
    return pl.pallas_call(
        final_kernel,
        out_shape=jax.ShapeDtypeStruct((PAIRS, HELD), F32),
        compiler_params=pltpu.CompilerParams(vmem_limit_bytes=16 << 20),
        name="final_sum",
    )(*parts, pick)


def store_pairs(move):
    pairs = []
    for z_lo in range(4):
        for x in range(4):
            pairs.append((node(x, z_lo, 0, 0, 0)[0], node(*move(x, z_lo), 0, 0, 0)[0]))
    return pairs


def all_pairs(move):
    pairs = []
    for z_lo in range(4):
        for x in range(4):
            for y in range(4):
                for z_hi in range(2):
                    for core in range(2):
                        dst = move(x, core)
                        if dst is None:
                            continue
                        s, g = node(x, z_lo, y, z_hi, core)
                        t, h = node(dst[0], z_lo, y, z_hi, dst[1])
                        pairs.append((s * 16 + g, t * 16 + h))
    return pairs


def along(value, move):
    return lax.ppermute(value, "group", group_pairs(move))


def fence_kernel(*refs):
    pass


def after(value, *others):
    hold = pl.BlockSpec(memory_space=pl.ANY)
    return pl.pallas_call(
        fence_kernel,
        out_shape=jax.ShapeDtypeStruct(value.shape, value.dtype),
        in_specs=[hold] * (1 + len(others)),
        out_specs=hold,
        input_output_aliases={0: 0},
        compiler_params=pltpu.CompilerParams(vmem_limit_bytes=1 << 20),
        name="fence",
    )(value, *others)


def far_blocks(value, earlier):
    far = along(value, lambda y, z, c: (y, z + 1, c))
    if earlier:
        far = after(far, *earlier)
    above = along(far, lambda y, z, c: (y - 1, z, c))
    below = along(far, lambda y, z, c: (y + 1, z, c))
    opposite = along(above, lambda y, z, c: (y - 1, z, c))
    return [far, below, above, opposite]


def own_blocks(value):
    groups = [[(y * 2 + z) * 2 + c for y in range(4)] for z in range(2) for c in range(2)]
    got = lax.all_gather(value, "group", axis=0, tiled=True, axis_index_groups=groups)
    return pltpu.with_memory_space_constraint(got.reshape(4, PAIRS, FEATURES), pltpu.HBM)


def over_x(bufs):
    def match(x, core):
        return x % 2 == core

    moves = (
        lambda x, c: (x + 2, c) if match(x, c) else (x + 1, 1 - c),
        lambda x, c: (x + 2, 1 - c) if match(x, c) else (x + 1, c),
        lambda x, c: (x, 1 - c) if match(x, c) else (x - 1, c),
        lambda x, c: None if match(x, c) else (x - 1, 1 - c),
    )
    return [lax.ppermute(b, ("store", "group"), all_pairs(m)) for b, m in zip(bufs, moves)]


def on_device(activations, out_grads, stored, lengths, store_ids):
    stored = stored.reshape(HELD, FEATURES)
    other = lax.ppermute(stored, "group", group_pairs(lambda y, z, c: (y, z, 1 - c)))
    pick = (store_ids[None, :] == jnp.arange(HELD, dtype=jnp.int32)[:, None]).astype(BF16)
    inputs = [
        pltpu.with_memory_space_constraint(v, pltpu.HBM) for v in (lengths, activations, out_grads)
    ]
    (a,) = query_grads(*inputs, ())
    b, both = query_grads(*inputs, (a,))
    own = own_blocks(both)
    parts = []
    far_a = far_blocks(a, ())
    far_b = far_blocks(b, far_a[1:])
    for n, fars in enumerate([far_a, far_b]):
        bufs = partial_scores(own, fars, stored, other, n)
        keep, *sends = cross_sum(*over_x(bufs), bufs[3])
        parts.append(keep)
        for k, send in enumerate(sends, 1):
            parts.append(lax.ppermute(send, "store", store_pairs(lambda x, z: (x, z + k))))
    return final_sum(parts, pick)


def solution(mesh):
    in_specs = (
        P("group", "store", None, None),
        P("group", "store", None, None),
        P("group", "store", None),
        P("group"),
        P("group"),
    )
    out_specs = P("store", "group")
    return jax.shard_map(
        on_device, mesh=mesh, in_specs=in_specs, out_specs=out_specs, check_vma=False
    )
```

```python
import functools

import jax
import jax.numpy as jnp
from jax import lax
from jax.experimental import pallas as pl
from jax.experimental.pallas import tpu as pltpu
from jax.sharding import PartitionSpec as P

CHUNKS = 2
PAIRS = 64
ROWS = PAIRS // CHUNKS
WIDTH = 64
SLOTS = 256
FEATURES = WIDTH * WIDTH
HELD = 768
STEP_PAIRS = 8
PITCH = 72
COLS = 256
F32 = jnp.float32
BF16 = jnp.bfloat16


def node(x, z_lo, y, z_hi, core):
    return (z_lo % 4) * 4 + x % 4, ((y % 4) * 2 + z_hi % 2) * 2 + core % 2


def group_pairs(move):
    pairs = []
    for y in range(4):
        for z_hi in range(2):
            for core in range(2):
                dst = move(y, z_hi, core)
                if dst is not None:
                    pairs.append((node(0, 0, y, z_hi, core)[1], node(0, 0, *dst)[1]))
    return pairs


def place():
    store, group = lax.axis_index("store"), lax.axis_index("group")
    return store % 4, store // 4, group // 4, (group // 2) % 2, group % 2


def grad_kernel(first, lengths_hbm, acts_hbm, grads_hbm, out_ref, acts_ref, grads_ref, lengths_ref, wide_ref, sems):
    def copies(n):
        src, dst = pl.ds(first + n * STEP_PAIRS, STEP_PAIRS), pl.ds(n * STEP_PAIRS, STEP_PAIRS)
        return (
            pltpu.make_async_copy(acts_hbm.at[src, 0], acts_ref.at[dst], sems.at[2 * n]),
            pltpu.make_async_copy(grads_hbm.at[src, 0], grads_ref.at[dst], sems.at[2 * n + 1]),
        )

    steps = ROWS // STEP_PAIRS
    lengths_copy = pltpu.make_async_copy(lengths_hbm, lengths_ref, sems.at[2 * steps])
    lengths_copy.start()
    for n in range(steps):
        for copy in copies(n):
            copy.start()
    lengths_copy.wait()
    slot = lax.broadcasted_iota(jnp.int32, (WIDTH, SLOTS), 1)
    for n in range(steps):
        for copy in copies(n):
            copy.wait()
        for p in range(n * STEP_PAIRS, (n + 1) * STEP_PAIRS):
            acts = acts_ref[p]
            acts = jnp.where(slot < lengths_ref[first + p], acts, jnp.zeros_like(acts))
            wide_ref[pl.ds(p * PITCH, WIDTH), :] = lax.dot_general(
                grads_ref[p],
                jnp.concatenate([acts, acts], axis=0),
                (((1,), (1,)), ((), ())),
                preferred_element_type=F32,
            )
    low = lax.broadcasted_iota(jnp.int32, (ROWS, 128), 1) < WIDTH
    for c in range(FEATURES // 128):
        even = wide_ref[pl.ds(2 * c, ROWS, stride=PITCH), :]
        odd = wide_ref[pl.ds(2 * c + 1, ROWS, stride=PITCH), :]
        out_ref[:, c * 128 : (c + 1) * 128] = jnp.where(low, even, odd).astype(BF16)


def query_grads(lengths, activations, out_grads, chunk):
    hbm = pl.BlockSpec(memory_space=pltpu.HBM)
    return pl.pallas_call(
        functools.partial(grad_kernel, chunk * ROWS),
        out_shape=jax.ShapeDtypeStruct((ROWS, FEATURES), BF16),
        in_specs=[hbm] * 3,
        scratch_shapes=[
            pltpu.VMEM((ROWS, WIDTH, SLOTS), BF16),
            pltpu.VMEM((ROWS, WIDTH, SLOTS), BF16),
            pltpu.SMEM((PAIRS,), jnp.int32),
            pltpu.VMEM((ROWS * PITCH, 128), F32),
            pltpu.SemaphoreType.DMA((2 * (ROWS // STEP_PAIRS) + 1,)),
        ],
        compiler_params=pltpu.CompilerParams(vmem_limit_bytes=16 << 20),
        name="query_grads",
    )(lengths, activations, out_grads)


def score_kernel(*refs):
    blocks, (mine_ref, other_ref), outs = refs[:8], refs[8:10], refs[10:14]
    rows_ref, sem = refs[14:]
    step = pl.program_id(0)
    x, _, y, z_hi, core = place()

    @pl.when(step == 0)
    def _():
        copies = [
            pltpu.make_async_copy(block, rows_ref.at[pl.ds(i * ROWS, ROWS)], sem.at[i])
            for i, block in enumerate(blocks)
        ]
        for copy in copies:
            copy.start()
        for copy in copies:
            copy.wait()

    def part(weights_ref, rel_core, tile):
        got = lax.dot_general(
            rows_ref[...],
            weights_ref[...],
            (((1,), (1,)), ((), ())),
            preferred_element_type=F32,
        ).astype(BF16)
        for rel_z in range(2):
            to_x = 2 * ((z_hi + rel_z) % 2) + core
            away = (to_x - x + 4) % 4
            if rel_core == 0:
                buf = jnp.where(away == 0, 3, jnp.where(away == 1, 1, jnp.where(away == 2, 0, 2)))
            else:
                buf = jnp.where(away == 0, 2, jnp.where(away == 1, 0, jnp.where(away == 2, 1, 3)))
            for b in range(4):

                @pl.when(buf == b)
                def _():
                    for j, dy in enumerate((0, 3, 1, 2)):
                        row = pl.multiple_of(((y + dy) % 4) * ROWS, ROWS)
                        at = (rel_z * 4 + j) * ROWS
                        outs[b][pl.ds(row, ROWS), tile * COLS : (tile + 1) * COLS] = got[at : at + ROWS]

    tiles = HELD // COLS
    for s in range(2 * tiles):

        @pl.when(step == s)
        def _():
            part(mine_ref if s < tiles else other_ref, s // tiles, s % tiles)


def partial_scores(blocks, mine, other):
    tiles = HELD // COLS
    out = pl.BlockSpec((4 * ROWS, HELD), lambda i: (0, 0))
    return pl.pallas_call(
        score_kernel,
        out_shape=[jax.ShapeDtypeStruct((4 * ROWS, HELD), BF16)] * 4,
        grid=(2 * tiles,),
        in_specs=[pl.BlockSpec(memory_space=pl.ANY)] * 8
        + [
            pl.BlockSpec((COLS, FEATURES), lambda i: (jnp.minimum(i, tiles - 1), 0)),
            pl.BlockSpec((COLS, FEATURES), lambda i: (jnp.maximum(i - tiles, 0), 0)),
        ],
        out_specs=[out] * 4,
        scratch_shapes=[
            pltpu.VMEM((8 * ROWS, FEATURES), BF16),
            pltpu.SemaphoreType.DMA((8,)),
        ],
        compiler_params=pltpu.CompilerParams(vmem_limit_bytes=18 << 20),
        cost_estimate=pl.CostEstimate(flops=1, bytes_accessed=1, transcendentals=0),
        name="partial_scores",
    )(*blocks, mine, other)


def cross_sum_kernel(a_ref, b_ref, c_ref, d_ref, own_ref, keep_ref, *outs):
    x, z_lo, _, _, core = place()
    match = (x % 2) == core
    for k in range(4):
        rows = pl.ds(pl.multiple_of(((z_lo + k) % 4) * ROWS, ROWS), ROWS)
        last = jnp.where(match, own_ref[rows, :].astype(F32), d_ref[rows, :].astype(F32))
        total = a_ref[rows, :].astype(F32) + b_ref[rows, :].astype(F32)
        total = total + (c_ref[rows, :].astype(F32) + last)
        if k == 0:
            keep_ref[...] = total
        else:
            outs[k - 1][...] = total.astype(BF16)


def cross_sum(*parts):
    return pl.pallas_call(
        cross_sum_kernel,
        out_shape=[jax.ShapeDtypeStruct((ROWS, HELD), F32)]
        + [jax.ShapeDtypeStruct((ROWS, HELD), BF16)] * 3,
        compiler_params=pltpu.CompilerParams(vmem_limit_bytes=16 << 20),
        name="cross_sum",
    )(*parts)


def final_kernel(*refs):
    pick_ref, out_ref = refs[-2:]
    totals = []
    for n in range(CHUNKS):
        keep, first, second, third = refs[4 * n : 4 * n + 4]
        total = keep[...] + first[...].astype(F32)
        totals.append(total + (second[...].astype(F32) + third[...].astype(F32)))
    total = jnp.concatenate(totals, axis=0)
    high = total.astype(BF16)
    rest = total - high.astype(F32)
    middle = rest.astype(BF16)
    low = (rest - middle.astype(F32)).astype(BF16)
    picked = lax.dot_general(
        jnp.concatenate([high, middle, low], axis=0),
        pick_ref[...],
        (((1,), (0,)), ((), ())),
        preferred_element_type=F32,
    )
    out_ref[...] = picked[:PAIRS] + (picked[PAIRS : 2 * PAIRS] + picked[2 * PAIRS :])


def final_sum(parts, pick):
    return pl.pallas_call(
        final_kernel,
        out_shape=jax.ShapeDtypeStruct((PAIRS, HELD), F32),
        compiler_params=pltpu.CompilerParams(vmem_limit_bytes=16 << 20),
        name="final_sum",
    )(*parts, pick)


def store_pairs(move):
    pairs = []
    for z_lo in range(4):
        for x in range(4):
            pairs.append((node(x, z_lo, 0, 0, 0)[0], node(*move(x, z_lo), 0, 0, 0)[0]))
    return pairs


def all_pairs(move):
    pairs = []
    for z_lo in range(4):
        for x in range(4):
            for y in range(4):
                for z_hi in range(2):
                    for core in range(2):
                        dst = move(x, core)
                        if dst is None:
                            continue
                        s, g = node(x, z_lo, y, z_hi, core)
                        t, h = node(dst[0], z_lo, y, z_hi, dst[1])
                        pairs.append((s * 16 + g, t * 16 + h))
    return pairs


def along(value, move):
    return lax.ppermute(value, "group", group_pairs(move))


def fence_kernel(*refs):
    pass


def after(values, *others):
    hold = pl.BlockSpec(memory_space=pl.ANY)
    return pl.pallas_call(
        fence_kernel,
        out_shape=[jax.ShapeDtypeStruct(v.shape, v.dtype) for v in values],
        in_specs=[hold] * (len(values) + len(others)),
        out_specs=[hold] * len(values),
        input_output_aliases={i: i for i in range(len(values))},
        compiler_params=pltpu.CompilerParams(vmem_limit_bytes=1 << 20),
        name="fence",
    )(*values, *others)


def up(value):
    return along(value, lambda y, z, c: (y + 1, z, c))


def down(value):
    return along(value, lambda y, z, c: (y - 1, z, c))


def beyond(value):
    return along(value, lambda y, z, c: (y, z + 1, c))


def gather_blocks(a, b, other):
    far_a = beyond(a)
    a_below, a_above = up(a), down(a)
    (b,) = after((b,), other)
    far_b = beyond(b)
    b_below, b_above = up(b), down(b)
    far_a, a_below = after((far_a, a_below), a_above, b_below, b_above)
    far_a_above, far_a_below = down(far_a), up(far_a)
    a_opposite = up(a_below)
    far_a_opposite = down(far_a_above)
    far_b, b_below = after((far_b, b_below), a_opposite, far_a_opposite, far_a_below)
    b_opposite = up(b_below)
    far_b_above, far_b_below = down(far_b), up(far_b)
    far_b_opposite = down(far_b_above)
    return (
        [a, a_below, a_above, a_opposite, far_a, far_a_below, far_a_above, far_a_opposite],
        [b, b_below, b_above, b_opposite, far_b, far_b_below, far_b_above, far_b_opposite],
    )


def over_x(bufs):
    def match(x, core):
        return x % 2 == core

    moves = (
        lambda x, c: (x + 2, c) if match(x, c) else (x + 1, 1 - c),
        lambda x, c: (x + 2, 1 - c) if match(x, c) else (x + 1, c),
        lambda x, c: (x, 1 - c) if match(x, c) else (x - 1, c),
        lambda x, c: None if match(x, c) else (x - 1, 1 - c),
    )
    return [lax.ppermute(b, ("store", "group"), all_pairs(m)) for b, m in zip(bufs, moves)]


def on_device(activations, out_grads, stored, lengths, store_ids):
    stored = stored.reshape(HELD, FEATURES)
    other = lax.ppermute(stored, "group", group_pairs(lambda y, z, c: (y, z, 1 - c)))
    pick = (store_ids[None, :] == jnp.arange(HELD, dtype=jnp.int32)[:, None]).astype(BF16)
    inputs = [
        pltpu.with_memory_space_constraint(v, pltpu.HBM) for v in (lengths, activations, out_grads)
    ]
    a, b = (query_grads(*inputs, n) for n in range(CHUNKS))
    parts, got = [], ()
    a_blocks, b_blocks = gather_blocks(a, b, other)
    for blocks in (a_blocks, b_blocks):
        blocks[-1:] = after(blocks[-1:], *got) if got else blocks[-1:]
        bufs = list(partial_scores(blocks, stored, other))
        if not got:
            bufs[1:2] = after(bufs[1:2], b_blocks[3], b_blocks[5])
        got = over_x(bufs)
        keep, *sends = cross_sum(*got, bufs[3])
        parts.append(keep)
        for k, send in enumerate(sends, 1):
            parts.append(lax.ppermute(send, "store", store_pairs(lambda x, z: (x, z + k))))
    return final_sum(parts, pick)


def solution(mesh):
    in_specs = (
        P("group", "store", None, None),
        P("group", "store", None, None),
        P("group", "store", None),
        P("group"),
        P("group"),
    )
    out_specs = P("store", "group")
    return jax.shard_map(
        on_device, mesh=mesh, in_specs=in_specs, out_specs=out_specs, check_vma=False
    )
```

```python
import functools

import jax
import jax.numpy as jnp
from jax import lax
from jax.experimental import pallas as pl
from jax.experimental.pallas import tpu as pltpu
from jax.sharding import PartitionSpec as P

CHUNKS = 2
PAIRS = 64
ROWS = PAIRS // CHUNKS
WIDTH = 64
SLOTS = 256
FEATURES = WIDTH * WIDTH
HELD = 768
STEP_PAIRS = 8
PITCH = 72
COLS = 256
F32 = jnp.float32
BF16 = jnp.bfloat16


def node(x, z_lo, y, z_hi, core):
    return (z_lo % 4) * 4 + x % 4, ((y % 4) * 2 + z_hi % 2) * 2 + core % 2


def group_pairs(move):
    pairs = []
    for y in range(4):
        for z_hi in range(2):
            for core in range(2):
                dst = move(y, z_hi, core)
                if dst is not None:
                    pairs.append((node(0, 0, y, z_hi, core)[1], node(0, 0, *dst)[1]))
    return pairs


def place():
    store, group = lax.axis_index("store"), lax.axis_index("group")
    return store % 4, store // 4, group // 4, (group // 2) % 2, group % 2


def grad_kernel(first, lengths_hbm, acts_hbm, grads_hbm, out_ref, acts_ref, grads_ref, lengths_ref, wide_ref, sems):
    def copies(n):
        src, dst = pl.ds(first + n * STEP_PAIRS, STEP_PAIRS), pl.ds(n * STEP_PAIRS, STEP_PAIRS)
        return (
            pltpu.make_async_copy(acts_hbm.at[src, 0], acts_ref.at[dst], sems.at[2 * n]),
            pltpu.make_async_copy(grads_hbm.at[src, 0], grads_ref.at[dst], sems.at[2 * n + 1]),
        )

    steps = ROWS // STEP_PAIRS
    lengths_copy = pltpu.make_async_copy(lengths_hbm, lengths_ref, sems.at[2 * steps])
    lengths_copy.start()
    for n in range(steps):
        for copy in copies(n):
            copy.start()
    lengths_copy.wait()
    slot = lax.broadcasted_iota(jnp.int32, (WIDTH, SLOTS), 1)
    for n in range(steps):
        for copy in copies(n):
            copy.wait()
        for p in range(n * STEP_PAIRS, (n + 1) * STEP_PAIRS):
            acts = acts_ref[p]
            acts = jnp.where(slot < lengths_ref[first + p], acts, jnp.zeros_like(acts))
            wide_ref[pl.ds(p * PITCH, WIDTH), :] = lax.dot_general(
                grads_ref[p],
                jnp.concatenate([acts, acts], axis=0),
                (((1,), (1,)), ((), ())),
                preferred_element_type=F32,
            )
    low = lax.broadcasted_iota(jnp.int32, (ROWS, 128), 1) < WIDTH
    for c in range(FEATURES // 128):
        even = wide_ref[pl.ds(2 * c, ROWS, stride=PITCH), :]
        odd = wide_ref[pl.ds(2 * c + 1, ROWS, stride=PITCH), :]
        out_ref[:, c * 128 : (c + 1) * 128] = jnp.where(low, even, odd).astype(BF16)


def query_grads(lengths, activations, out_grads, chunk):
    hbm = pl.BlockSpec(memory_space=pltpu.HBM)
    return pl.pallas_call(
        functools.partial(grad_kernel, chunk * ROWS),
        out_shape=jax.ShapeDtypeStruct((ROWS, FEATURES), BF16),
        in_specs=[hbm] * 3,
        scratch_shapes=[
            pltpu.VMEM((ROWS, WIDTH, SLOTS), BF16),
            pltpu.VMEM((ROWS, WIDTH, SLOTS), BF16),
            pltpu.SMEM((PAIRS,), jnp.int32),
            pltpu.VMEM((ROWS * PITCH, 128), F32),
            pltpu.SemaphoreType.DMA((2 * (ROWS // STEP_PAIRS) + 1,)),
        ],
        compiler_params=pltpu.CompilerParams(vmem_limit_bytes=16 << 20),
        name="query_grads",
    )(lengths, activations, out_grads)


def score_kernel(*refs):
    blocks, held, outs, rows_ref = refs[:8], refs[8:10], refs[10:14], refs[14]
    x, _, y, z_hi, core = place()
    for i, block in enumerate(blocks):
        rows_ref[i * ROWS : (i + 1) * ROWS, :] = block[...]
    for rel_core in range(2):
        for tile in range(HELD // COLS):
            cols = slice(tile * COLS, (tile + 1) * COLS)
            got = lax.dot_general(
                rows_ref[...],
                held[rel_core][cols, :],
                (((1,), (1,)), ((), ())),
                preferred_element_type=F32,
            ).astype(BF16)
            for rel_z in range(2):
                to_x = 2 * ((z_hi + rel_z) % 2) + core
                away = (to_x - x + 4) % 4
                if rel_core == 0:
                    buf = jnp.where(away == 0, 3, jnp.where(away == 1, 1, jnp.where(away == 2, 0, 2)))
                else:
                    buf = jnp.where(away == 0, 2, jnp.where(away == 1, 0, jnp.where(away == 2, 1, 3)))
                for b in range(4):

                    @pl.when(buf == b)
                    def _():
                        for j, dy in enumerate((0, 3, 1, 2)):
                            row = pl.multiple_of(((y + dy) % 4) * ROWS, ROWS)
                            at = (rel_z * 4 + j) * ROWS
                            outs[b][pl.ds(row, ROWS), cols] = got[at : at + ROWS]


def partial_scores(blocks, mine, other):
    return pl.pallas_call(
        score_kernel,
        out_shape=[jax.ShapeDtypeStruct((4 * ROWS, HELD), BF16)] * 4,
        in_specs=[pl.BlockSpec(memory_space=pltpu.VMEM)] * 10,
        out_specs=[pl.BlockSpec(memory_space=pltpu.VMEM)] * 4,
        scratch_shapes=[pltpu.VMEM((8 * ROWS, FEATURES), BF16)],
        compiler_params=pltpu.CompilerParams(vmem_limit_bytes=24 << 20),
        cost_estimate=pl.CostEstimate(flops=1, bytes_accessed=1, transcendentals=0),
        name="partial_scores",
    )(*blocks, mine, other)


def cross_sum_kernel(a_ref, b_ref, c_ref, d_ref, own_ref, keep_ref, *outs):
    x, z_lo, _, _, core = place()
    match = (x % 2) == core
    for k in range(4):
        rows = pl.ds(pl.multiple_of(((z_lo + k) % 4) * ROWS, ROWS), ROWS)
        last = jnp.where(match, own_ref[rows, :].astype(F32), d_ref[rows, :].astype(F32))
        total = a_ref[rows, :].astype(F32) + b_ref[rows, :].astype(F32)
        total = total + (c_ref[rows, :].astype(F32) + last)
        if k == 0:
            keep_ref[...] = total
        else:
            outs[k - 1][...] = total.astype(BF16)


def cross_sum(*parts):
    return pl.pallas_call(
        cross_sum_kernel,
        out_shape=[jax.ShapeDtypeStruct((ROWS, HELD), F32)]
        + [jax.ShapeDtypeStruct((ROWS, HELD), BF16)] * 3,
        compiler_params=pltpu.CompilerParams(vmem_limit_bytes=16 << 20),
        name="cross_sum",
    )(*parts)


def final_kernel(*refs):
    pick_ref, out_ref = refs[-2:]
    totals = []
    for n in range(CHUNKS):
        keep, first, second, third = refs[4 * n : 4 * n + 4]
        total = keep[...] + first[...].astype(F32)
        totals.append(total + (second[...].astype(F32) + third[...].astype(F32)))
    total = jnp.concatenate(totals, axis=0)
    high = total.astype(BF16)
    rest = total - high.astype(F32)
    middle = rest.astype(BF16)
    low = (rest - middle.astype(F32)).astype(BF16)
    picked = lax.dot_general(
        jnp.concatenate([high, middle, low], axis=0),
        pick_ref[...],
        (((1,), (0,)), ((), ())),
        preferred_element_type=F32,
    )
    out_ref[...] = picked[:PAIRS] + (picked[PAIRS : 2 * PAIRS] + picked[2 * PAIRS :])


def final_sum(parts, pick):
    return pl.pallas_call(
        final_kernel,
        out_shape=jax.ShapeDtypeStruct((PAIRS, HELD), F32),
        compiler_params=pltpu.CompilerParams(vmem_limit_bytes=16 << 20),
        name="final_sum",
    )(*parts, pick)


def store_pairs(move):
    pairs = []
    for z_lo in range(4):
        for x in range(4):
            pairs.append((node(x, z_lo, 0, 0, 0)[0], node(*move(x, z_lo), 0, 0, 0)[0]))
    return pairs


def all_pairs(move):
    pairs = []
    for z_lo in range(4):
        for x in range(4):
            for y in range(4):
                for z_hi in range(2):
                    for core in range(2):
                        dst = move(x, core)
                        if dst is None:
                            continue
                        s, g = node(x, z_lo, y, z_hi, core)
                        t, h = node(dst[0], z_lo, y, z_hi, dst[1])
                        pairs.append((s * 16 + g, t * 16 + h))
    return pairs


def along(value, move):
    return lax.ppermute(value, "group", group_pairs(move))


def fence_kernel(*refs):
    pass


def after(values, *others):
    hold = pl.BlockSpec(memory_space=pl.ANY)
    return pl.pallas_call(
        fence_kernel,
        out_shape=[jax.ShapeDtypeStruct(v.shape, v.dtype) for v in values],
        in_specs=[hold] * (len(values) + len(others)),
        out_specs=[hold] * len(values),
        input_output_aliases={i: i for i in range(len(values))},
        compiler_params=pltpu.CompilerParams(vmem_limit_bytes=1 << 20),
        name="fence",
    )(*values, *others)


def up(value):
    return along(value, lambda y, z, c: (y + 1, z, c))


def down(value):
    return along(value, lambda y, z, c: (y - 1, z, c))


def beyond(value):
    return along(value, lambda y, z, c: (y, z + 1, c))


def first_scores(a, b, stored, other):
    far_a = beyond(a)
    a_below, a_above = up(a), down(a)
    (b,) = after((b,), other)
    far_b = beyond(b)
    b_below, b_above = up(b), down(b)
    far_a, a_below = after((far_a, a_below), a_above, b_below, b_above)
    a_opposite = up(a_below)
    far_a_above, far_a_below = down(far_a), up(far_a)
    far_a_opposite = down(far_a_above)
    far_b, b_below = after((far_b, b_below), a_opposite, far_a_opposite, far_a_below)
    b_opposite = up(b_below)
    far_b_above, far_b_below = down(far_b), up(far_b)
    a_blocks = [a, a_below, a_above, a_opposite, far_a, far_a_below, far_a_above, far_a_opposite]
    a_bufs = list(partial_scores(a_blocks, stored, other))
    (far_b_above,) = after((far_b_above,), a_bufs[3])
    far_b_opposite = down(far_b_above)
    a_bufs[0:1] = after(a_bufs[0:1], b_opposite, far_b_below)
    b_blocks = [b, b_below, b_above, b_opposite, far_b, far_b_below, far_b_above, far_b_opposite]
    return a_bufs, b_blocks


def over_x(bufs):
    def match(x, core):
        return x % 2 == core

    moves = (
        lambda x, c: (x + 2, c) if match(x, c) else (x + 1, 1 - c),
        lambda x, c: (x + 2, 1 - c) if match(x, c) else (x + 1, c),
        lambda x, c: (x, 1 - c) if match(x, c) else (x - 1, c),
        lambda x, c: None if match(x, c) else (x - 1, 1 - c),
    )
    return [lax.ppermute(b, ("store", "group"), all_pairs(m)) for b, m in zip(bufs, moves)]


def on_device(activations, out_grads, stored, lengths, store_ids):
    stored = stored.reshape(HELD, FEATURES)
    other = lax.ppermute(stored, "group", group_pairs(lambda y, z, c: (y, z, 1 - c)))
    pick = (store_ids[None, :] == jnp.arange(HELD, dtype=jnp.int32)[:, None]).astype(BF16)
    inputs = [
        pltpu.with_memory_space_constraint(v, pltpu.HBM) for v in (lengths, activations, out_grads)
    ]
    a, b = (query_grads(*inputs, n) for n in range(CHUNKS))
    a_bufs, b_blocks = first_scores(a, b, stored, other)
    a_got = over_x(a_bufs)
    b_bufs = list(partial_scores(b_blocks, stored, other))
    b_bufs[:3] = after(b_bufs[:3], *a_got)
    b_got = over_x(b_bufs)
    parts = []
    for got, bufs in ((a_got, a_bufs), (b_got, b_bufs)):
        keep, *sends = cross_sum(*got, bufs[3])
        parts.append(keep)
        for k, send in enumerate(sends, 1):
            parts.append(lax.ppermute(send, "store", store_pairs(lambda x, z: (x, z + k))))
    return final_sum(parts, pick)


def solution(mesh):
    in_specs = (
        P("group", "store", None, None),
        P("group", "store", None, None),
        P("group", "store", None),
        P("group"),
        P("group"),
    )
    out_specs = P("store", "group")
    return jax.shard_map(
        on_device, mesh=mesh, in_specs=in_specs, out_specs=out_specs, check_vma=False
    )
```

```python
import functools

import jax
import jax.numpy as jnp
from jax import lax
from jax.experimental import pallas as pl
from jax.experimental.pallas import tpu as pltpu
from jax.sharding import PartitionSpec as P

CHUNKS = 2
PAIRS = 64
ROWS = PAIRS // CHUNKS
WIDTH = 64
SLOTS = 256
FEATURES = WIDTH * WIDTH
HELD = 768
STEP_PAIRS = 8
PITCH = 72
DEPTH = 512
F32 = jnp.float32
BF16 = jnp.bfloat16


def node(x, z_lo, y, z_hi, core):
    return (z_lo % 4) * 4 + x % 4, ((y % 4) * 2 + z_hi % 2) * 2 + core % 2


def group_pairs(move):
    pairs = []
    for y in range(4):
        for z_hi in range(2):
            for core in range(2):
                dst = move(y, z_hi, core)
                if dst is not None:
                    pairs.append((node(0, 0, y, z_hi, core)[1], node(0, 0, *dst)[1]))
    return pairs


def place():
    store, group = lax.axis_index("store"), lax.axis_index("group")
    return store % 4, store // 4, group // 4, (group // 2) % 2, group % 2


def grad_kernel(first, lengths_hbm, acts_hbm, grads_hbm, out_ref, acts_ref, grads_ref, lengths_ref, wide_ref, sems):
    def copies(n):
        src, dst = pl.ds(first + n * STEP_PAIRS, STEP_PAIRS), pl.ds(n * STEP_PAIRS, STEP_PAIRS)
        return (
            pltpu.make_async_copy(acts_hbm.at[src, 0], acts_ref.at[dst], sems.at[2 * n]),
            pltpu.make_async_copy(grads_hbm.at[src, 0], grads_ref.at[dst], sems.at[2 * n + 1]),
        )

    steps = ROWS // STEP_PAIRS
    lengths_copy = pltpu.make_async_copy(lengths_hbm, lengths_ref, sems.at[2 * steps])
    lengths_copy.start()
    for n in range(steps):
        for copy in copies(n):
            copy.start()
    lengths_copy.wait()
    slot = lax.broadcasted_iota(jnp.int32, (WIDTH, SLOTS), 1)
    for n in range(steps):
        for copy in copies(n):
            copy.wait()
        for p in range(n * STEP_PAIRS, (n + 1) * STEP_PAIRS):
            acts = acts_ref[p]
            acts = jnp.where(slot < lengths_ref[first + p], acts, jnp.zeros_like(acts))
            wide_ref[pl.ds(p * PITCH, WIDTH), :] = lax.dot_general(
                grads_ref[p],
                jnp.concatenate([acts, acts], axis=0),
                (((1,), (1,)), ((), ())),
                preferred_element_type=F32,
            )
    low = lax.broadcasted_iota(jnp.int32, (ROWS, 128), 1) < WIDTH
    for c in range(FEATURES // 128):
        even = wide_ref[pl.ds(2 * c, ROWS, stride=PITCH), :]
        odd = wide_ref[pl.ds(2 * c + 1, ROWS, stride=PITCH), :]
        out_ref[:, c * 128 : (c + 1) * 128] = jnp.where(low, even, odd).astype(BF16)


def query_grads(lengths, activations, out_grads, chunk):
    hbm = pl.BlockSpec(memory_space=pltpu.HBM)
    return pl.pallas_call(
        functools.partial(grad_kernel, chunk * ROWS),
        out_shape=jax.ShapeDtypeStruct((ROWS, FEATURES), BF16),
        in_specs=[hbm] * 3,
        scratch_shapes=[
            pltpu.VMEM((ROWS, WIDTH, SLOTS), BF16),
            pltpu.VMEM((ROWS, WIDTH, SLOTS), BF16),
            pltpu.SMEM((PAIRS,), jnp.int32),
            pltpu.VMEM((ROWS * PITCH, 128), F32),
            pltpu.SemaphoreType.DMA((2 * (ROWS // STEP_PAIRS) + 1,)),
        ],
        compiler_params=pltpu.CompilerParams(vmem_limit_bytes=16 << 20),
        name="query_grads",
    )(lengths, activations, out_grads)


def score_kernel(*refs):
    blocks, held, outs, (rows_ref, total_ref) = refs[:8], refs[8:10], refs[10:14], refs[14:]
    x, _, y, z_hi, core = place()
    for i, block in enumerate(blocks):
        to_z = (y + (0, 3, 1, 2)[i % 4]) % 4
        row = pl.multiple_of((i // 4) * 4 * ROWS + to_z * ROWS, ROWS)
        rows_ref[pl.ds(row, ROWS), :] = block[...]
    for rel_core in range(2):
        for k in range(0, FEATURES, DEPTH):
            got = lax.dot_general(
                held[rel_core][:, k : k + DEPTH],
                rows_ref[:, k : k + DEPTH],
                (((1,), (1,)), ((), ())),
                preferred_element_type=F32,
            )
            total_ref[...] = got if k == 0 else total_ref[...] + got
        for rel_z in range(2):
            to_x = 2 * ((z_hi + rel_z) % 2) + core
            away = (to_x - x + 4) % 4
            if rel_core == 0:
                buf = jnp.where(away == 0, 3, jnp.where(away == 1, 1, jnp.where(away == 2, 0, 2)))
            else:
                buf = jnp.where(away == 0, 2, jnp.where(away == 1, 0, jnp.where(away == 2, 1, 3)))
            for b in range(4):

                @pl.when(buf == b)
                def _():
                    cols = slice(rel_z * 4 * ROWS, (rel_z + 1) * 4 * ROWS)
                    outs[b][...] = total_ref[:, cols].astype(BF16)


def partial_scores(blocks, mine, other):
    return pl.pallas_call(
        score_kernel,
        out_shape=[jax.ShapeDtypeStruct((HELD, 4 * ROWS), BF16)] * 4,
        in_specs=[pl.BlockSpec(memory_space=pltpu.VMEM)] * 10,
        out_specs=[pl.BlockSpec(memory_space=pltpu.VMEM)] * 4,
        scratch_shapes=[
            pltpu.VMEM((8 * ROWS, FEATURES), BF16),
            pltpu.VMEM((HELD, 8 * ROWS), F32),
        ],
        compiler_params=pltpu.CompilerParams(vmem_limit_bytes=24 << 20),
        cost_estimate=pl.CostEstimate(flops=1, bytes_accessed=1, transcendentals=0),
        name="partial_scores",
    )(*blocks, mine, other)


def cross_sum_kernel(*refs):
    keep_ref, *outs, turned_ref = refs[5 * CHUNKS :]
    x, z_lo, _, _, core = place()
    match = (x % 2) == core
    for n in range(CHUNKS):
        a_ref, b_ref, c_ref, d_ref, own_ref = refs[5 * n : 5 * n + 5]
        last = jnp.where(match, own_ref[...].astype(F32), d_ref[...].astype(F32))
        total = a_ref[...].astype(F32) + b_ref[...].astype(F32)
        total = total + (c_ref[...].astype(F32) + last)
        turned_ref[...] = total.T
        for k in range(4):
            rows = pl.ds(pl.multiple_of(((z_lo + k) % 4) * ROWS, ROWS), ROWS)
            part = turned_ref[rows, :]
            at = slice(n * ROWS, (n + 1) * ROWS)
            if k == 0:
                keep_ref[at, :] = part
            else:
                outs[k - 1][at, :] = part.astype(BF16)


def cross_sum(parts):
    return pl.pallas_call(
        cross_sum_kernel,
        out_shape=[jax.ShapeDtypeStruct((PAIRS, HELD), F32)]
        + [jax.ShapeDtypeStruct((PAIRS, HELD), BF16)] * 3,
        scratch_shapes=[pltpu.VMEM((4 * ROWS, HELD), F32)],
        compiler_params=pltpu.CompilerParams(vmem_limit_bytes=16 << 20),
        name="cross_sum",
    )(*parts)


def final_kernel(keep_ref, first_ref, second_ref, third_ref, pick_ref, out_ref):
    total = keep_ref[...] + first_ref[...].astype(F32)
    total = total + (second_ref[...].astype(F32) + third_ref[...].astype(F32))
    high = total.astype(BF16)
    rest = total - high.astype(F32)
    middle = rest.astype(BF16)
    low = (rest - middle.astype(F32)).astype(BF16)
    picked = lax.dot_general(
        jnp.concatenate([high, middle, low], axis=0),
        pick_ref[...],
        (((1,), (0,)), ((), ())),
        preferred_element_type=F32,
    )
    out_ref[...] = picked[:PAIRS] + (picked[PAIRS : 2 * PAIRS] + picked[2 * PAIRS :])


def final_sum(parts, pick):
    return pl.pallas_call(
        final_kernel,
        out_shape=jax.ShapeDtypeStruct((PAIRS, HELD), F32),
        compiler_params=pltpu.CompilerParams(vmem_limit_bytes=16 << 20),
        name="final_sum",
    )(*parts, pick)


def store_pairs(move):
    pairs = []
    for z_lo in range(4):
        for x in range(4):
            pairs.append((node(x, z_lo, 0, 0, 0)[0], node(*move(x, z_lo), 0, 0, 0)[0]))
    return pairs


def all_pairs(move):
    pairs = []
    for z_lo in range(4):
        for x in range(4):
            for y in range(4):
                for z_hi in range(2):
                    for core in range(2):
                        dst = move(x, core)
                        if dst is None:
                            continue
                        s, g = node(x, z_lo, y, z_hi, core)
                        t, h = node(dst[0], z_lo, y, z_hi, dst[1])
                        pairs.append((s * 16 + g, t * 16 + h))
    return pairs


def along(value, move):
    return lax.ppermute(value, "group", group_pairs(move))


def fence_kernel(*refs):
    pass


def after(values, *others):
    hold = pl.BlockSpec(memory_space=pl.ANY)
    return pl.pallas_call(
        fence_kernel,
        out_shape=[jax.ShapeDtypeStruct(v.shape, v.dtype) for v in values],
        in_specs=[hold] * (len(values) + len(others)),
        out_specs=[hold] * len(values),
        input_output_aliases={i: i for i in range(len(values))},
        compiler_params=pltpu.CompilerParams(vmem_limit_bytes=1 << 20),
        name="fence",
    )(*values, *others)


def up(value):
    return along(value, lambda y, z, c: (y + 1, z, c))


def down(value):
    return along(value, lambda y, z, c: (y - 1, z, c))


def beyond(value):
    return along(value, lambda y, z, c: (y, z + 1, c))


def first_scores(a, b, stored, other):
    far_a = beyond(a)
    a_below, a_above = up(a), down(a)
    (b,) = after((b,), other)
    far_b = beyond(b)
    b_below, b_above = up(b), down(b)
    far_a, a_below = after((far_a, a_below), a_above, b_below, b_above)
    a_opposite = up(a_below)
    far_a_above, far_a_below = down(far_a), up(far_a)
    far_a_opposite = down(far_a_above)
    far_b, b_below = after((far_b, b_below), a_opposite, far_a_opposite, far_a_below)
    b_opposite = up(b_below)
    far_b_above, far_b_below = down(far_b), up(far_b)
    a_blocks = [a, a_below, a_above, a_opposite, far_a, far_a_below, far_a_above, far_a_opposite]
    a_bufs = list(partial_scores(a_blocks, stored, other))
    (far_b_above,) = after((far_b_above,), a_bufs[3])
    far_b_opposite = down(far_b_above)
    a_bufs[0:1] = after(a_bufs[0:1], b_opposite, far_b_below)
    b_blocks = [b, b_below, b_above, b_opposite, far_b, far_b_below, far_b_above, far_b_opposite]
    return a_bufs, b_blocks


def over_x(bufs):
    def match(x, core):
        return x % 2 == core

    moves = (
        lambda x, c: (x + 2, c) if match(x, c) else (x + 1, 1 - c),
        lambda x, c: (x + 2, 1 - c) if match(x, c) else (x + 1, c),
        lambda x, c: (x, 1 - c) if match(x, c) else (x - 1, c),
        lambda x, c: None if match(x, c) else (x - 1, 1 - c),
    )
    return [lax.ppermute(b, ("store", "group"), all_pairs(m)) for b, m in zip(bufs, moves)]


def on_device(activations, out_grads, stored, lengths, store_ids):
    stored = stored.reshape(HELD, FEATURES)
    other = lax.ppermute(stored, "group", group_pairs(lambda y, z, c: (y, z, 1 - c)))
    pick = (store_ids[None, :] == jnp.arange(HELD, dtype=jnp.int32)[:, None]).astype(BF16)
    inputs = [
        pltpu.with_memory_space_constraint(v, pltpu.HBM) for v in (lengths, activations, out_grads)
    ]
    a, b = (query_grads(*inputs, n) for n in range(CHUNKS))
    a_bufs, b_blocks = first_scores(a, b, stored, other)
    a_got = over_x(a_bufs)
    b_bufs = list(partial_scores(b_blocks, stored, other))
    b_bufs[:3] = after(b_bufs[:3], *a_got)
    b_got = over_x(b_bufs)
    keep, *sends = cross_sum([*a_got, a_bufs[3], *b_got, b_bufs[3]])
    parts = [keep]
    for k, send in enumerate(sends, 1):
        parts.append(lax.ppermute(send, "store", store_pairs(lambda x, z: (x, z + k))))
    return final_sum(parts, pick)


def solution(mesh):
    in_specs = (
        P("group", "store", None, None),
        P("group", "store", None, None),
        P("group", "store", None),
        P("group"),
        P("group"),
    )
    out_specs = P("store", "group")
    return jax.shard_map(
        on_device, mesh=mesh, in_specs=in_specs, out_specs=out_specs, check_vma=False
    )
```

```python
import functools

import jax
import jax.numpy as jnp
from jax import lax
from jax.experimental import pallas as pl
from jax.experimental.pallas import tpu as pltpu
from jax.sharding import PartitionSpec as P

CHUNKS = 2
PAIRS = 64
ROWS = PAIRS // CHUNKS
WIDTH = 64
SLOTS = 256
FEATURES = WIDTH * WIDTH
HELD = 768
STEP_PAIRS = 8
PITCH = 72
COLS = 256
F32 = jnp.float32
BF16 = jnp.bfloat16


def node(x, z_lo, y, z_hi, core):
    return (z_lo % 4) * 4 + x % 4, ((y % 4) * 2 + z_hi % 2) * 2 + core % 2


def group_pairs(move):
    pairs = []
    for y in range(4):
        for z_hi in range(2):
            for core in range(2):
                dst = move(y, z_hi, core)
                if dst is not None:
                    pairs.append((node(0, 0, y, z_hi, core)[1], node(0, 0, *dst)[1]))
    return pairs


def place():
    store, group = lax.axis_index("store"), lax.axis_index("group")
    return store % 4, store // 4, group // 4, (group // 2) % 2, group % 2


def grad_kernel(first, lengths_hbm, acts_hbm, grads_hbm, out_ref, acts_ref, grads_ref, lengths_ref, wide_ref, sems):
    def copies(n):
        src, dst = pl.ds(first + n * STEP_PAIRS, STEP_PAIRS), pl.ds(n * STEP_PAIRS, STEP_PAIRS)
        return (
            pltpu.make_async_copy(acts_hbm.at[src, 0], acts_ref.at[dst], sems.at[2 * n]),
            pltpu.make_async_copy(grads_hbm.at[src, 0], grads_ref.at[dst], sems.at[2 * n + 1]),
        )

    steps = ROWS // STEP_PAIRS
    lengths_copy = pltpu.make_async_copy(lengths_hbm, lengths_ref, sems.at[2 * steps])
    lengths_copy.start()
    for n in range(steps):
        for copy in copies(n):
            copy.start()
    lengths_copy.wait()
    slot = lax.broadcasted_iota(jnp.int32, (WIDTH, SLOTS), 1)
    for n in range(steps):
        for copy in copies(n):
            copy.wait()
        for p in range(n * STEP_PAIRS, (n + 1) * STEP_PAIRS):
            acts = acts_ref[p]
            acts = jnp.where(slot < lengths_ref[first + p], acts, jnp.zeros_like(acts))
            wide_ref[pl.ds(p * PITCH, WIDTH), :] = lax.dot_general(
                grads_ref[p],
                jnp.concatenate([acts, acts], axis=0),
                (((1,), (1,)), ((), ())),
                preferred_element_type=F32,
            )
    low = lax.broadcasted_iota(jnp.int32, (ROWS, 128), 1) < WIDTH
    for c in range(FEATURES // 128):
        even = wide_ref[pl.ds(2 * c, ROWS, stride=PITCH), :]
        odd = wide_ref[pl.ds(2 * c + 1, ROWS, stride=PITCH), :]
        out_ref[:, c * 128 : (c + 1) * 128] = jnp.where(low, even, odd).astype(BF16)


def query_grads(lengths, activations, out_grads, chunk):
    hbm = pl.BlockSpec(memory_space=pltpu.HBM)
    return pl.pallas_call(
        functools.partial(grad_kernel, chunk * ROWS),
        out_shape=jax.ShapeDtypeStruct((ROWS, FEATURES), BF16),
        in_specs=[hbm] * 3,
        scratch_shapes=[
            pltpu.VMEM((ROWS, WIDTH, SLOTS), BF16),
            pltpu.VMEM((ROWS, WIDTH, SLOTS), BF16),
            pltpu.SMEM((PAIRS,), jnp.int32),
            pltpu.VMEM((ROWS * PITCH, 128), F32),
            pltpu.SemaphoreType.DMA((2 * (ROWS // STEP_PAIRS) + 1,)),
        ],
        compiler_params=pltpu.CompilerParams(vmem_limit_bytes=16 << 20),
        name="query_grads",
    )(lengths, activations, out_grads)


def score_kernel(*refs):
    blocks, (mine_ref, other_ref), outs = refs[:8], refs[8:10], refs[10:14]
    rows_ref, sem = refs[14:]
    step = pl.program_id(0)
    x, _, y, z_hi, core = place()

    @pl.when(step == 0)
    def _():
        copies = [
            pltpu.make_async_copy(block, rows_ref.at[pl.ds(i * ROWS, ROWS)], sem.at[i])
            for i, block in enumerate(blocks)
        ]
        for copy in copies:
            copy.start()
        for copy in copies:
            copy.wait()

    def part(weights_ref, rel_core, tile):
        got = lax.dot_general(
            rows_ref[...],
            weights_ref[...],
            (((1,), (1,)), ((), ())),
            preferred_element_type=F32,
        ).astype(BF16)
        for rel_z in range(2):
            to_x = 2 * ((z_hi + rel_z) % 2) + core
            away = (to_x - x + 4) % 4
            if rel_core == 0:
                buf = jnp.where(away == 0, 1, jnp.where(away == 1, 3, jnp.where(away == 2, 2, 0)))
            else:
                buf = jnp.where(away == 0, 0, jnp.where(away == 1, 2, jnp.where(away == 2, 3, 1)))
            for b in range(4):

                @pl.when(buf == b)
                def _():
                    for j, dy in enumerate((0, 3, 1, 2)):
                        row = pl.multiple_of(((y + dy) % 4) * ROWS, ROWS)
                        at = (rel_z * 4 + j) * ROWS
                        outs[b][pl.ds(row, ROWS), tile * COLS : (tile + 1) * COLS] = got[at : at + ROWS]

    tiles = HELD // COLS
    for s in range(2 * tiles):

        @pl.when(step == s)
        def _():
            part(mine_ref if s < tiles else other_ref, s // tiles, s % tiles)


def partial_scores(blocks, mine, other):
    tiles = HELD // COLS
    out = pl.BlockSpec((4 * ROWS, HELD), lambda i: (0, 0))
    return pl.pallas_call(
        score_kernel,
        out_shape=[jax.ShapeDtypeStruct((4 * ROWS, HELD), BF16)] * 4,
        grid=(2 * tiles,),
        in_specs=[pl.BlockSpec(memory_space=pl.ANY)] * 8
        + [
            pl.BlockSpec((COLS, FEATURES), lambda i: (jnp.minimum(i, tiles - 1), 0)),
            pl.BlockSpec((COLS, FEATURES), lambda i: (jnp.maximum(i - tiles, 0), 0)),
        ],
        out_specs=[out] * 4,
        scratch_shapes=[
            pltpu.VMEM((8 * ROWS, FEATURES), BF16),
            pltpu.SemaphoreType.DMA((8,)),
        ],
        compiler_params=pltpu.CompilerParams(vmem_limit_bytes=18 << 20),
        cost_estimate=pl.CostEstimate(flops=1, bytes_accessed=1, transcendentals=0),
        name="partial_scores",
    )(*blocks, mine, other)


def cross_sum_kernel(c_ref, d_ref, a_ref, b_ref, own_ref, keep_ref, *outs):
    x, z_lo, _, _, core = place()
    match = (x % 2) == core
    for k in range(4):
        rows = pl.ds(pl.multiple_of(((z_lo + k) % 4) * ROWS, ROWS), ROWS)
        last = jnp.where(match, own_ref[rows, :].astype(F32), d_ref[rows, :].astype(F32))
        total = a_ref[rows, :].astype(F32) + b_ref[rows, :].astype(F32)
        total = total + (c_ref[rows, :].astype(F32) + last)
        if k == 0:
            keep_ref[...] = total
        else:
            outs[k - 1][...] = total.astype(BF16)


def cross_sum(*parts):
    return pl.pallas_call(
        cross_sum_kernel,
        out_shape=[jax.ShapeDtypeStruct((ROWS, HELD), F32)]
        + [jax.ShapeDtypeStruct((ROWS, HELD), BF16)] * 3,
        compiler_params=pltpu.CompilerParams(vmem_limit_bytes=16 << 20),
        name="cross_sum",
    )(*parts)


def final_kernel(*refs):
    pick_ref, out_ref = refs[-2:]
    totals = []
    for n in range(CHUNKS):
        keep, first, second, third = refs[4 * n : 4 * n + 4]
        total = keep[...] + first[...].astype(F32)
        totals.append(total + (second[...].astype(F32) + third[...].astype(F32)))
    total = jnp.concatenate(totals, axis=0)
    high = total.astype(BF16)
    rest = total - high.astype(F32)
    middle = rest.astype(BF16)
    low = (rest - middle.astype(F32)).astype(BF16)
    picked = lax.dot_general(
        jnp.concatenate([high, middle, low], axis=0),
        pick_ref[...],
        (((1,), (0,)), ((), ())),
        preferred_element_type=F32,
    )
    out_ref[...] = picked[:PAIRS] + (picked[PAIRS : 2 * PAIRS] + picked[2 * PAIRS :])


def final_sum(parts, pick):
    return pl.pallas_call(
        final_kernel,
        out_shape=jax.ShapeDtypeStruct((PAIRS, HELD), F32),
        compiler_params=pltpu.CompilerParams(vmem_limit_bytes=16 << 20),
        name="final_sum",
    )(*parts, pick)


def store_pairs(move):
    pairs = []
    for z_lo in range(4):
        for x in range(4):
            pairs.append((node(x, z_lo, 0, 0, 0)[0], node(*move(x, z_lo), 0, 0, 0)[0]))
    return pairs


def all_pairs(move):
    pairs = []
    for z_lo in range(4):
        for x in range(4):
            for y in range(4):
                for z_hi in range(2):
                    for core in range(2):
                        dst = move(x, core)
                        if dst is None:
                            continue
                        s, g = node(x, z_lo, y, z_hi, core)
                        t, h = node(dst[0], z_lo, y, z_hi, dst[1])
                        pairs.append((s * 16 + g, t * 16 + h))
    return pairs


def along(value, move):
    return lax.ppermute(value, "group", group_pairs(move))


def fence_kernel(*refs):
    pass


def after(values, *others):
    hold = pl.BlockSpec(memory_space=pl.ANY)
    return pl.pallas_call(
        fence_kernel,
        out_shape=[jax.ShapeDtypeStruct(v.shape, v.dtype) for v in values],
        in_specs=[hold] * (len(values) + len(others)),
        out_specs=[hold] * len(values),
        input_output_aliases={i: i for i in range(len(values))},
        compiler_params=pltpu.CompilerParams(vmem_limit_bytes=1 << 20),
        name="fence",
    )(*values, *others)


def up(value):
    return along(value, lambda y, z, c: (y + 1, z, c))


def down(value):
    return along(value, lambda y, z, c: (y - 1, z, c))


def beyond(value):
    return along(value, lambda y, z, c: (y, z + 1, c))


def first_scores(a, b, stored, other):
    far_a = beyond(a)
    a_below, a_above = up(a), down(a)
    (b,) = after((b,), other)
    far_b = beyond(b)
    b_below, b_above = up(b), down(b)
    far_a, a_below = after((far_a, a_below), a_above, b_below, b_above)
    a_opposite = up(a_below)
    far_a_above, far_a_below = down(far_a), up(far_a)
    far_a_above, far_b = after((far_a_above, far_b))
    far_a_opposite = down(far_a_above)
    far_b_above, far_b_below = down(far_b), up(far_b)
    b_opposite = up(b_below)
    a_blocks = [a, a_below, a_above, a_opposite, far_a, far_a_below, far_a_above, far_a_opposite]
    a_bufs = list(partial_scores(a_blocks, stored, other))
    (far_b_above,) = after((far_b_above,), a_bufs[1])
    far_b_opposite = down(far_b_above)
    a_bufs[3:] = after(a_bufs[3:], b_opposite, far_b_below)
    b_blocks = [b, b_below, b_above, b_opposite, far_b, far_b_below, far_b_above, far_b_opposite]
    return a_bufs, b_blocks


def over_x(bufs):
    def match(x, core):
        return x % 2 == core

    moves = (
        lambda x, c: (x, 1 - c) if match(x, c) else (x - 1, c),
        lambda x, c: None if match(x, c) else (x - 1, 1 - c),
        lambda x, c: (x + 2, c) if match(x, c) else (x + 1, 1 - c),
        lambda x, c: (x + 2, 1 - c) if match(x, c) else (x + 1, c),
    )
    return [lax.ppermute(b, ("store", "group"), all_pairs(m)) for b, m in zip(bufs, moves)]


def on_device(activations, out_grads, stored, lengths, store_ids):
    stored = stored.reshape(HELD, FEATURES)
    other = lax.ppermute(stored, "group", group_pairs(lambda y, z, c: (y, z, 1 - c)))
    pick = (store_ids[None, :] == jnp.arange(HELD, dtype=jnp.int32)[:, None]).astype(BF16)
    inputs = [
        pltpu.with_memory_space_constraint(v, pltpu.HBM) for v in (lengths, activations, out_grads)
    ]
    a, b = (query_grads(*inputs, n) for n in range(CHUNKS))
    a_bufs, b_blocks = first_scores(a, b, stored, other)
    a_got = over_x(a_bufs)
    b_bufs = list(partial_scores(b_blocks, stored, other))
    b_bufs = after(b_bufs, *a_got)
    b_got = over_x(b_bufs)
    parts = []
    for got, bufs in ((a_got, a_bufs), (b_got, b_bufs)):
        keep, *sends = cross_sum(*got, bufs[1])
        parts.append(keep)
        for k, send in enumerate(sends, 1):
            parts.append(lax.ppermute(send, "store", store_pairs(lambda x, z: (x, z + k))))
    return final_sum(parts, pick)


def solution(mesh):
    in_specs = (
        P("group", "store", None, None),
        P("group", "store", None, None),
        P("group", "store", None),
        P("group"),
        P("group"),
    )
    out_specs = P("store", "group")
    return jax.shard_map(
        on_device, mesh=mesh, in_specs=in_specs, out_specs=out_specs, check_vma=False
    )
```

```python
import functools

import jax
import jax.numpy as jnp
from jax import lax
from jax.experimental import pallas as pl
from jax.experimental.pallas import tpu as pltpu
from jax.sharding import PartitionSpec as P

CHUNKS = 2
PAIRS = 64
ROWS = PAIRS // CHUNKS
WIDTH = 64
SLOTS = 256
FEATURES = WIDTH * WIDTH
HELD = 768
STEP_PAIRS = 8
PITCH = 72
COLS = 256
F32 = jnp.float32
BF16 = jnp.bfloat16


def node(x, z_lo, y, z_hi, core):
    return (z_lo % 4) * 4 + x % 4, ((y % 4) * 2 + z_hi % 2) * 2 + core % 2


def group_pairs(move):
    pairs = []
    for y in range(4):
        for z_hi in range(2):
            for core in range(2):
                dst = move(y, z_hi, core)
                if dst is not None:
                    pairs.append((node(0, 0, y, z_hi, core)[1], node(0, 0, *dst)[1]))
    return pairs


def place():
    store, group = lax.axis_index("store"), lax.axis_index("group")
    return store % 4, store // 4, group // 4, (group // 2) % 2, group % 2


def grad_kernel(first, lengths_hbm, acts_hbm, grads_hbm, out_ref, acts_ref, grads_ref, lengths_ref, wide_ref, sems):
    def copies(n):
        src, dst = pl.ds(first + n * STEP_PAIRS, STEP_PAIRS), pl.ds(n * STEP_PAIRS, STEP_PAIRS)
        return (
            pltpu.make_async_copy(acts_hbm.at[src, 0], acts_ref.at[dst], sems.at[2 * n]),
            pltpu.make_async_copy(grads_hbm.at[src, 0], grads_ref.at[dst], sems.at[2 * n + 1]),
        )

    steps = ROWS // STEP_PAIRS
    lengths_copy = pltpu.make_async_copy(lengths_hbm, lengths_ref, sems.at[2 * steps])
    lengths_copy.start()
    for n in range(steps):
        for copy in copies(n):
            copy.start()
    lengths_copy.wait()
    slot = lax.broadcasted_iota(jnp.int32, (WIDTH, SLOTS), 1)
    for n in range(steps):
        for copy in copies(n):
            copy.wait()
        for p in range(n * STEP_PAIRS, (n + 1) * STEP_PAIRS):
            acts = acts_ref[p]
            acts = jnp.where(slot < lengths_ref[first + p], acts, jnp.zeros_like(acts))
            wide_ref[pl.ds(p * PITCH, WIDTH), :] = lax.dot_general(
                grads_ref[p],
                jnp.concatenate([acts, acts], axis=0),
                (((1,), (1,)), ((), ())),
                preferred_element_type=F32,
            )
    low = lax.broadcasted_iota(jnp.int32, (ROWS, 128), 1) < WIDTH
    for c in range(FEATURES // 128):
        even = wide_ref[pl.ds(2 * c, ROWS, stride=PITCH), :]
        odd = wide_ref[pl.ds(2 * c + 1, ROWS, stride=PITCH), :]
        out_ref[:, c * 128 : (c + 1) * 128] = jnp.where(low, even, odd).astype(BF16)


def query_grads(lengths, activations, out_grads, chunk):
    hbm = pl.BlockSpec(memory_space=pltpu.HBM)
    return pl.pallas_call(
        functools.partial(grad_kernel, chunk * ROWS),
        out_shape=jax.ShapeDtypeStruct((ROWS, FEATURES), BF16),
        in_specs=[hbm] * 3,
        scratch_shapes=[
            pltpu.VMEM((ROWS, WIDTH, SLOTS), BF16),
            pltpu.VMEM((ROWS, WIDTH, SLOTS), BF16),
            pltpu.SMEM((PAIRS,), jnp.int32),
            pltpu.VMEM((ROWS * PITCH, 128), F32),
            pltpu.SemaphoreType.DMA((2 * (ROWS // STEP_PAIRS) + 1,)),
        ],
        compiler_params=pltpu.CompilerParams(vmem_limit_bytes=16 << 20),
        name="query_grads",
    )(lengths, activations, out_grads)


def score_kernel(*refs):
    blocks, (mine_ref, other_ref), outs = refs[:8], refs[8:10], refs[10:14]
    rows_ref, sem = refs[14:]
    step = pl.program_id(0)
    x, _, y, z_hi, core = place()

    @pl.when(step == 0)
    def _():
        copies = [
            pltpu.make_async_copy(block, rows_ref.at[pl.ds(i * ROWS, ROWS)], sem.at[i])
            for i, block in enumerate(blocks)
        ]
        for copy in copies:
            copy.start()
        for copy in copies:
            copy.wait()

    def part(weights_ref, rel_core, tile):
        got = lax.dot_general(
            rows_ref[...],
            weights_ref[...],
            (((1,), (1,)), ((), ())),
            preferred_element_type=F32,
        ).astype(BF16)
        for rel_z in range(2):
            to_x = 2 * ((z_hi + rel_z) % 2) + core
            away = (to_x - x + 4) % 4
            if rel_core == 0:
                buf = jnp.where(away == 0, 1, jnp.where(away == 1, 3, jnp.where(away == 2, 2, 0)))
            else:
                buf = jnp.where(away == 0, 0, jnp.where(away == 1, 2, jnp.where(away == 2, 3, 1)))
            for b in range(4):

                @pl.when(buf == b)
                def _():
                    for j, dy in enumerate((0, 3, 1, 2)):
                        row = pl.multiple_of(((y + dy) % 4) * ROWS, ROWS)
                        at = (rel_z * 4 + j) * ROWS
                        outs[b][pl.ds(row, ROWS), tile * COLS : (tile + 1) * COLS] = got[at : at + ROWS]

    tiles = HELD // COLS
    for s in range(2 * tiles):

        @pl.when(step == s)
        def _():
            part(mine_ref if s < tiles else other_ref, s // tiles, s % tiles)


def partial_scores(blocks, mine, other):
    tiles = HELD // COLS
    out = pl.BlockSpec((4 * ROWS, HELD), lambda i: (0, 0))
    return pl.pallas_call(
        score_kernel,
        out_shape=[jax.ShapeDtypeStruct((4 * ROWS, HELD), BF16)] * 4,
        grid=(2 * tiles,),
        in_specs=[pl.BlockSpec(memory_space=pl.ANY)] * 8
        + [
            pl.BlockSpec((COLS, FEATURES), lambda i: (jnp.minimum(i, tiles - 1), 0)),
            pl.BlockSpec((COLS, FEATURES), lambda i: (jnp.maximum(i - tiles, 0), 0)),
        ],
        out_specs=[out] * 4,
        scratch_shapes=[
            pltpu.VMEM((8 * ROWS, FEATURES), BF16),
            pltpu.SemaphoreType.DMA((8,)),
        ],
        compiler_params=pltpu.CompilerParams(vmem_limit_bytes=18 << 20),
        cost_estimate=pl.CostEstimate(flops=1, bytes_accessed=1, transcendentals=0),
        name="partial_scores",
    )(*blocks, mine, other)


def cross_sum_kernel(b_ref, c_ref, a_ref, d_ref, own_ref, keep_ref, *outs):
    x, z_lo, _, _, core = place()
    match = (x % 2) == core
    for k in range(4):
        rows = pl.ds(pl.multiple_of(((z_lo + k) % 4) * ROWS, ROWS), ROWS)
        near = own_ref[rows, :].astype(F32) + b_ref[rows, :].astype(F32)
        last = jnp.where(match, near, d_ref[rows, :].astype(F32))
        total = (a_ref[rows, :].astype(F32) + c_ref[rows, :].astype(F32)) + last
        if k == 0:
            keep_ref[...] = total
        else:
            outs[k - 1][...] = total.astype(BF16)


def cross_sum(*parts):
    return pl.pallas_call(
        cross_sum_kernel,
        out_shape=[jax.ShapeDtypeStruct((ROWS, HELD), F32)]
        + [jax.ShapeDtypeStruct((ROWS, HELD), BF16)] * 3,
        compiler_params=pltpu.CompilerParams(vmem_limit_bytes=16 << 20),
        name="cross_sum",
    )(*parts)


def final_kernel(*refs):
    pick_ref, out_ref = refs[-2:]
    totals = []
    for n in range(CHUNKS):
        keep, first, second, third = refs[4 * n : 4 * n + 4]
        total = keep[...] + first[...].astype(F32)
        totals.append(total + (second[...].astype(F32) + third[...].astype(F32)))
    total = jnp.concatenate(totals, axis=0)
    high = total.astype(BF16)
    rest = total - high.astype(F32)
    middle = rest.astype(BF16)
    low = (rest - middle.astype(F32)).astype(BF16)
    picked = lax.dot_general(
        jnp.concatenate([high, middle, low], axis=0),
        pick_ref[...],
        (((1,), (0,)), ((), ())),
        preferred_element_type=F32,
    )
    out_ref[...] = picked[:PAIRS] + (picked[PAIRS : 2 * PAIRS] + picked[2 * PAIRS :])


def final_sum(parts, pick):
    return pl.pallas_call(
        final_kernel,
        out_shape=jax.ShapeDtypeStruct((PAIRS, HELD), F32),
        compiler_params=pltpu.CompilerParams(vmem_limit_bytes=16 << 20),
        name="final_sum",
    )(*parts, pick)


def store_pairs(move):
    pairs = []
    for z_lo in range(4):
        for x in range(4):
            pairs.append((node(x, z_lo, 0, 0, 0)[0], node(*move(x, z_lo), 0, 0, 0)[0]))
    return pairs


def all_pairs(move):
    pairs = []
    for z_lo in range(4):
        for x in range(4):
            for y in range(4):
                for z_hi in range(2):
                    for core in range(2):
                        dst = move(x, core)
                        if dst is None:
                            continue
                        s, g = node(x, z_lo, y, z_hi, core)
                        t, h = node(dst[0], z_lo, y, z_hi, dst[1])
                        pairs.append((s * 16 + g, t * 16 + h))
    return pairs


def along(value, move):
    return lax.ppermute(value, "group", group_pairs(move))


def fence_kernel(*refs):
    pass


def after(values, *others):
    hold = pl.BlockSpec(memory_space=pl.ANY)
    return pl.pallas_call(
        fence_kernel,
        out_shape=[jax.ShapeDtypeStruct(v.shape, v.dtype) for v in values],
        in_specs=[hold] * (len(values) + len(others)),
        out_specs=[hold] * len(values),
        input_output_aliases={i: i for i in range(len(values))},
        compiler_params=pltpu.CompilerParams(vmem_limit_bytes=1 << 20),
        name="fence",
    )(*values, *others)


def up(value):
    return along(value, lambda y, z, c: (y + 1, z, c))


def down(value):
    return along(value, lambda y, z, c: (y - 1, z, c))


def beyond(value):
    return along(value, lambda y, z, c: (y, z + 1, c))


def first_scores(a, b, stored, other):
    far_a = beyond(a)
    a_below, a_above = up(a), down(a)
    (b,) = after((b,), other)
    far_b = beyond(b)
    b_below, b_above = up(b), down(b)
    far_a, a_below = after((far_a, a_below), a_above, b_below, b_above)
    a_opposite = up(a_below)
    far_a_above, far_a_below = down(far_a), up(far_a)
    far_a_opposite = down(far_a_above)
    far_b, b_below = after((far_b, b_below), a_opposite, far_a_opposite, far_a_below)
    b_opposite = up(b_below)
    far_b_above, far_b_below = down(far_b), up(far_b)
    a_blocks = [a, a_below, a_above, a_opposite, far_a, far_a_below, far_a_above, far_a_opposite]
    a_bufs = list(partial_scores(a_blocks, stored, other))
    (far_b_above,) = after((far_b_above,), a_bufs[1])
    far_b_opposite = down(far_b_above)
    a_bufs[2:3] = after(a_bufs[2:3], b_opposite, far_b_below)
    b_blocks = [b, b_below, b_above, b_opposite, far_b, far_b_below, far_b_above, far_b_opposite]
    return a_bufs, b_blocks


def join_kernel(send_ref, got_ref, out_ref):
    x, _, _, _, core = place()
    got = jnp.where((x % 2) == core, 0.0, got_ref[...].astype(F32))
    out_ref[...] = (send_ref[...].astype(F32) + got).astype(BF16)


def join(send, got):
    return pl.pallas_call(
        join_kernel,
        out_shape=jax.ShapeDtypeStruct(send.shape, BF16),
        compiler_params=pltpu.CompilerParams(vmem_limit_bytes=16 << 20),
        name="join",
    )(send, got)


def over_x(bufs):
    def send(value, move):
        return lax.ppermute(value, ("store", "group"), all_pairs(move))

    def match(x, core):
        return x % 2 == core

    got_b = send(bufs[3], lambda x, c: (x - 1, c) if match(x, c) else (x + 1, c))
    got_c = send(bufs[0], lambda x, c: (x, 1 - c) if match(x, c) else (x - 1, c))
    got_a = send(bufs[2], lambda x, c: (x + 2, c) if match(x, c) else (x + 1, 1 - c))
    joined = join(bufs[1], got_b)
    got_d = send(joined, lambda x, c: None if match(x, c) else (x - 1, 1 - c))
    return [got_b, got_c, got_a, got_d]


def on_device(activations, out_grads, stored, lengths, store_ids):
    stored = stored.reshape(HELD, FEATURES)
    other = lax.ppermute(stored, "group", group_pairs(lambda y, z, c: (y, z, 1 - c)))
    pick = (store_ids[None, :] == jnp.arange(HELD, dtype=jnp.int32)[:, None]).astype(BF16)
    inputs = [
        pltpu.with_memory_space_constraint(v, pltpu.HBM) for v in (lengths, activations, out_grads)
    ]
    a, b = (query_grads(*inputs, n) for n in range(CHUNKS))
    a_bufs, b_blocks = first_scores(a, b, stored, other)
    a_got = over_x(a_bufs)
    b_bufs = list(partial_scores(b_blocks, stored, other))
    b_bufs = after(b_bufs, *a_got[:3])
    b_got = over_x(b_bufs)
    parts = []
    for got, bufs in ((a_got, a_bufs), (b_got, b_bufs)):
        keep, *sends = cross_sum(*got, bufs[1])
        parts.append(keep)
        for k, send in enumerate(sends, 1):
            parts.append(lax.ppermute(send, "store", store_pairs(lambda x, z: (x, z + k))))
    return final_sum(parts, pick)


def solution(mesh):
    in_specs = (
        P("group", "store", None, None),
        P("group", "store", None, None),
        P("group", "store", None),
        P("group"),
        P("group"),
    )
    out_specs = P("store", "group")
    return jax.shard_map(
        on_device, mesh=mesh, in_specs=in_specs, out_specs=out_specs, check_vma=False
    )
```

```python
import functools

import jax
import jax.numpy as jnp
from jax import lax
from jax.experimental import pallas as pl
from jax.experimental.pallas import tpu as pltpu
from jax.sharding import PartitionSpec as P

CHUNKS = 2
PAIRS = 64
ROWS = PAIRS // CHUNKS
WIDTH = 64
SLOTS = 256
FEATURES = WIDTH * WIDTH
HELD = 768
STEP_PAIRS = 8
PITCH = 72
COLS = 256
F32 = jnp.float32
BF16 = jnp.bfloat16


def node(x, z_lo, y, z_hi, core):
    return (z_lo % 4) * 4 + x % 4, ((y % 4) * 2 + z_hi % 2) * 2 + core % 2


def group_pairs(move):
    pairs = []
    for y in range(4):
        for z_hi in range(2):
            for core in range(2):
                dst = move(y, z_hi, core)
                if dst is not None:
                    pairs.append((node(0, 0, y, z_hi, core)[1], node(0, 0, *dst)[1]))
    return pairs


def place():
    store, group = lax.axis_index("store"), lax.axis_index("group")
    return store % 4, store // 4, group // 4, (group // 2) % 2, group % 2


def grad_kernel(first, lengths_hbm, acts_hbm, grads_hbm, out_ref, acts_ref, grads_ref, lengths_ref, wide_ref, sems):
    def copies(n):
        src, dst = pl.ds(first + n * STEP_PAIRS, STEP_PAIRS), pl.ds(n * STEP_PAIRS, STEP_PAIRS)
        return (
            pltpu.make_async_copy(acts_hbm.at[src, 0], acts_ref.at[dst], sems.at[2 * n]),
            pltpu.make_async_copy(grads_hbm.at[src, 0], grads_ref.at[dst], sems.at[2 * n + 1]),
        )

    steps = ROWS // STEP_PAIRS
    lengths_copy = pltpu.make_async_copy(lengths_hbm, lengths_ref, sems.at[2 * steps])
    lengths_copy.start()
    for n in range(steps):
        for copy in copies(n):
            copy.start()
    lengths_copy.wait()
    slot = lax.broadcasted_iota(jnp.int32, (WIDTH, SLOTS), 1)
    for n in range(steps):
        for copy in copies(n):
            copy.wait()
        for p in range(n * STEP_PAIRS, (n + 1) * STEP_PAIRS):
            acts = acts_ref[p]
            acts = jnp.where(slot < lengths_ref[first + p], acts, jnp.zeros_like(acts))
            wide_ref[pl.ds(p * PITCH, WIDTH), :] = lax.dot_general(
                grads_ref[p],
                jnp.concatenate([acts, acts], axis=0),
                (((1,), (1,)), ((), ())),
                preferred_element_type=F32,
            )
    low = lax.broadcasted_iota(jnp.int32, (ROWS, 128), 1) < WIDTH
    for c in range(FEATURES // 128):
        even = wide_ref[pl.ds(2 * c, ROWS, stride=PITCH), :]
        odd = wide_ref[pl.ds(2 * c + 1, ROWS, stride=PITCH), :]
        out_ref[:, c * 128 : (c + 1) * 128] = jnp.where(low, even, odd).astype(BF16)


def query_grads(lengths, activations, out_grads, chunk):
    hbm = pl.BlockSpec(memory_space=pltpu.HBM)
    return pl.pallas_call(
        functools.partial(grad_kernel, chunk * ROWS),
        out_shape=jax.ShapeDtypeStruct((ROWS, FEATURES), BF16),
        in_specs=[hbm] * 3,
        scratch_shapes=[
            pltpu.VMEM((ROWS, WIDTH, SLOTS), BF16),
            pltpu.VMEM((ROWS, WIDTH, SLOTS), BF16),
            pltpu.SMEM((PAIRS,), jnp.int32),
            pltpu.VMEM((ROWS * PITCH, 128), F32),
            pltpu.SemaphoreType.DMA((2 * (ROWS // STEP_PAIRS) + 1,)),
        ],
        compiler_params=pltpu.CompilerParams(vmem_limit_bytes=16 << 20),
        name="query_grads",
    )(lengths, activations, out_grads)


def score_kernel(*refs):
    blocks, (mine_ref, other_ref), outs = refs[:8], refs[8:10], refs[10:14]
    rows_ref, cols_ref, sem = refs[14:]
    step = pl.program_id(0)
    x, _, y, z_hi, core = place()

    @pl.when(step == 0)
    def _():
        copies = [
            pltpu.make_async_copy(block, rows_ref.at[pl.ds(i * ROWS, ROWS)], sem.at[i])
            for i, block in enumerate(blocks)
        ]
        for copy in copies:
            copy.start()
        for copy in copies:
            copy.wait()
        for k in range(0, FEATURES, COLS):
            cols_ref[k : k + COLS, :] = rows_ref[:, k : k + COLS].T

    def part(weights_ref, rel_core, tile):
        got = lax.dot_general(
            weights_ref[...],
            cols_ref[...],
            (((1,), (0,)), ((), ())),
            preferred_element_type=F32,
        ).T.astype(BF16)
        for rel_z in range(2):
            to_x = 2 * ((z_hi + rel_z) % 2) + core
            away = (to_x - x + 4) % 4
            if rel_core == 0:
                buf = jnp.where(away == 0, 1, jnp.where(away == 1, 3, jnp.where(away == 2, 2, 0)))
            else:
                buf = jnp.where(away == 0, 0, jnp.where(away == 1, 2, jnp.where(away == 2, 3, 1)))
            for b in range(4):

                @pl.when(buf == b)
                def _():
                    for j, dy in enumerate((0, 3, 1, 2)):
                        row = pl.multiple_of(((y + dy) % 4) * ROWS, ROWS)
                        at = (rel_z * 4 + j) * ROWS
                        outs[b][pl.ds(row, ROWS), tile * COLS : (tile + 1) * COLS] = got[at : at + ROWS]

    tiles = HELD // COLS
    for s in range(2 * tiles):

        @pl.when(step == s)
        def _():
            part(mine_ref if s < tiles else other_ref, s // tiles, s % tiles)


def partial_scores(blocks, mine, other):
    tiles = HELD // COLS
    out = pl.BlockSpec((4 * ROWS, HELD), lambda i: (0, 0))
    return pl.pallas_call(
        score_kernel,
        out_shape=[jax.ShapeDtypeStruct((4 * ROWS, HELD), BF16)] * 4,
        grid=(2 * tiles,),
        in_specs=[pl.BlockSpec(memory_space=pl.ANY)] * 8
        + [
            pl.BlockSpec((COLS, FEATURES), lambda i: (jnp.minimum(i, tiles - 1), 0)),
            pl.BlockSpec((COLS, FEATURES), lambda i: (jnp.maximum(i - tiles, 0), 0)),
        ],
        out_specs=[out] * 4,
        scratch_shapes=[
            pltpu.VMEM((8 * ROWS, FEATURES), BF16),
            pltpu.VMEM((FEATURES, 8 * ROWS), BF16),
            pltpu.SemaphoreType.DMA((8,)),
        ],
        compiler_params=pltpu.CompilerParams(vmem_limit_bytes=20 << 20),
        cost_estimate=pl.CostEstimate(flops=1, bytes_accessed=1, transcendentals=0),
        name="partial_scores",
    )(*blocks, mine, other)


def cross_sum_kernel(b_ref, c_ref, a_ref, d_ref, own_ref, keep_ref, *outs):
    x, z_lo, _, _, core = place()
    match = (x % 2) == core
    for k in range(4):
        rows = pl.ds(pl.multiple_of(((z_lo + k) % 4) * ROWS, ROWS), ROWS)
        near = own_ref[rows, :].astype(F32) + b_ref[rows, :].astype(F32)
        last = jnp.where(match, near, d_ref[rows, :].astype(F32))
        total = (a_ref[rows, :].astype(F32) + c_ref[rows, :].astype(F32)) + last
        if k == 0:
            keep_ref[...] = total
        else:
            outs[k - 1][...] = total.astype(BF16)


def cross_sum(*parts):
    return pl.pallas_call(
        cross_sum_kernel,
        out_shape=[jax.ShapeDtypeStruct((ROWS, HELD), F32)]
        + [jax.ShapeDtypeStruct((ROWS, HELD), BF16)] * 3,
        compiler_params=pltpu.CompilerParams(vmem_limit_bytes=16 << 20),
        name="cross_sum",
    )(*parts)


def final_kernel(*refs):
    pick_ref, out_ref = refs[-2:]
    totals = []
    for n in range(CHUNKS):
        keep, first, second, third = refs[4 * n : 4 * n + 4]
        total = keep[...] + first[...].astype(F32)
        totals.append(total + (second[...].astype(F32) + third[...].astype(F32)))
    total = jnp.concatenate(totals, axis=0)
    high = total.astype(BF16)
    rest = total - high.astype(F32)
    middle = rest.astype(BF16)
    low = (rest - middle.astype(F32)).astype(BF16)
    picked = lax.dot_general(
        jnp.concatenate([high, middle, low], axis=0),
        pick_ref[...],
        (((1,), (0,)), ((), ())),
        preferred_element_type=F32,
    )
    out_ref[...] = picked[:PAIRS] + (picked[PAIRS : 2 * PAIRS] + picked[2 * PAIRS :])


def final_sum(parts, pick):
    return pl.pallas_call(
        final_kernel,
        out_shape=jax.ShapeDtypeStruct((PAIRS, HELD), F32),
        compiler_params=pltpu.CompilerParams(vmem_limit_bytes=16 << 20),
        name="final_sum",
    )(*parts, pick)


def store_pairs(move):
    pairs = []
    for z_lo in range(4):
        for x in range(4):
            pairs.append((node(x, z_lo, 0, 0, 0)[0], node(*move(x, z_lo), 0, 0, 0)[0]))
    return pairs


def all_pairs(move):
    pairs = []
    for z_lo in range(4):
        for x in range(4):
            for y in range(4):
                for z_hi in range(2):
                    for core in range(2):
                        dst = move(x, core)
                        if dst is None:
                            continue
                        s, g = node(x, z_lo, y, z_hi, core)
                        t, h = node(dst[0], z_lo, y, z_hi, dst[1])
                        pairs.append((s * 16 + g, t * 16 + h))
    return pairs


def along(value, move):
    return lax.ppermute(value, "group", group_pairs(move))


def fence_kernel(*refs):
    pass


def after(values, *others):
    hold = pl.BlockSpec(memory_space=pl.ANY)
    return pl.pallas_call(
        fence_kernel,
        out_shape=[jax.ShapeDtypeStruct(v.shape, v.dtype) for v in values],
        in_specs=[hold] * (len(values) + len(others)),
        out_specs=[hold] * len(values),
        input_output_aliases={i: i for i in range(len(values))},
        compiler_params=pltpu.CompilerParams(vmem_limit_bytes=1 << 20),
        name="fence",
    )(*values, *others)


def up(value):
    return along(value, lambda y, z, c: (y + 1, z, c))


def down(value):
    return along(value, lambda y, z, c: (y - 1, z, c))


def beyond(value):
    return along(value, lambda y, z, c: (y, z + 1, c))


def first_scores(a, b, stored, other):
    far_a = beyond(a)
    a_below, a_above = up(a), down(a)
    (b,) = after((b,), other)
    far_b = beyond(b)
    b_below, b_above = up(b), down(b)
    far_a, a_below = after((far_a, a_below), a_above, b_below, b_above)
    a_opposite = up(a_below)
    far_a_above, far_a_below = down(far_a), up(far_a)
    far_a_opposite = down(far_a_above)
    far_b, b_below = after((far_b, b_below), a_opposite, far_a_opposite, far_a_below)
    b_opposite = up(b_below)
    far_b_above, far_b_below = down(far_b), up(far_b)
    a_blocks = [a, a_below, a_above, a_opposite, far_a, far_a_below, far_a_above, far_a_opposite]
    a_bufs = list(partial_scores(a_blocks, stored, other))
    (far_b_above,) = after((far_b_above,), a_bufs[1])
    far_b_opposite = down(far_b_above)
    a_bufs[0:1] = after(a_bufs[0:1], b_opposite, far_b_below)
    b_blocks = [b, b_below, b_above, b_opposite, far_b, far_b_below, far_b_above, far_b_opposite]
    return a_bufs, b_blocks


def join_kernel(send_ref, got_ref, out_ref):
    x, _, _, _, core = place()
    got = jnp.where((x % 2) == core, 0.0, got_ref[...].astype(F32))
    out_ref[...] = (send_ref[...].astype(F32) + got).astype(BF16)


def join(send, got):
    return pl.pallas_call(
        join_kernel,
        out_shape=jax.ShapeDtypeStruct(send.shape, BF16),
        compiler_params=pltpu.CompilerParams(vmem_limit_bytes=16 << 20),
        name="join",
    )(send, got)


def over_x(bufs):
    def send(value, move):
        return lax.ppermute(value, ("store", "group"), all_pairs(move))

    def match(x, core):
        return x % 2 == core

    got_b = send(bufs[3], lambda x, c: (x - 1, c) if match(x, c) else (x + 1, c))
    got_c = send(bufs[0], lambda x, c: (x, 1 - c) if match(x, c) else (x - 1, c))
    got_a = send(bufs[2], lambda x, c: (x + 2, c) if match(x, c) else (x + 1, 1 - c))
    joined = join(bufs[1], got_b)
    got_d = send(joined, lambda x, c: None if match(x, c) else (x - 1, 1 - c))
    return [got_b, got_c, got_a, got_d]


def on_device(activations, out_grads, stored, lengths, store_ids):
    stored = stored.reshape(HELD, FEATURES)
    other = lax.ppermute(stored, "group", group_pairs(lambda y, z, c: (y, z, 1 - c)))
    pick = (store_ids[None, :] == jnp.arange(HELD, dtype=jnp.int32)[:, None]).astype(BF16)
    inputs = [
        pltpu.with_memory_space_constraint(v, pltpu.HBM) for v in (lengths, activations, out_grads)
    ]
    a, b = (query_grads(*inputs, n) for n in range(CHUNKS))
    a_bufs, b_blocks = first_scores(a, b, stored, other)
    a_got = over_x(a_bufs)
    b_bufs = list(partial_scores(b_blocks, stored, other))
    b_bufs = after(b_bufs, *a_got)
    b_got = over_x(b_bufs)
    parts = []
    for got, bufs in ((a_got, a_bufs), (b_got, b_bufs)):
        keep, *sends = cross_sum(*got, bufs[1])
        parts.append(keep)
        for k, send in enumerate(sends, 1):
            parts.append(lax.ppermute(send, "store", store_pairs(lambda x, z: (x, z + k))))
    return final_sum(parts, pick)


def solution(mesh):
    in_specs = (
        P("group", "store", None, None),
        P("group", "store", None, None),
        P("group", "store", None),
        P("group"),
        P("group"),
    )
    out_specs = P("store", "group")
    return jax.shard_map(
        on_device, mesh=mesh, in_specs=in_specs, out_specs=out_specs, check_vma=False
    )
```

```python
import functools

import jax
import jax.numpy as jnp
from jax import lax
from jax.experimental import pallas as pl
from jax.experimental.pallas import tpu as pltpu
from jax.sharding import PartitionSpec as P

CHUNKS = 2
PAIRS = 64
ROWS = PAIRS // CHUNKS
WIDTH = 64
SLOTS = 256
FEATURES = WIDTH * WIDTH
HELD = 768
STEP_PAIRS = 8
PITCH = 72
COLS = 256
F32 = jnp.float32
BF16 = jnp.bfloat16


def node(x, z_lo, y, z_hi, core):
    return (z_lo % 4) * 4 + x % 4, ((y % 4) * 2 + z_hi % 2) * 2 + core % 2


def group_pairs(move):
    pairs = []
    for y in range(4):
        for z_hi in range(2):
            for core in range(2):
                dst = move(y, z_hi, core)
                if dst is not None:
                    pairs.append((node(0, 0, y, z_hi, core)[1], node(0, 0, *dst)[1]))
    return pairs


def place():
    store, group = lax.axis_index("store"), lax.axis_index("group")
    return store % 4, store // 4, group // 4, (group // 2) % 2, group % 2


def grad_kernel(first, lengths_hbm, acts_hbm, grads_hbm, out_ref, acts_ref, grads_ref, lengths_ref, wide_ref, sems):
    def copies(n):
        src, dst = pl.ds(first + n * STEP_PAIRS, STEP_PAIRS), pl.ds(n * STEP_PAIRS, STEP_PAIRS)
        return (
            pltpu.make_async_copy(acts_hbm.at[src, 0], acts_ref.at[dst], sems.at[2 * n]),
            pltpu.make_async_copy(grads_hbm.at[src, 0], grads_ref.at[dst], sems.at[2 * n + 1]),
        )

    steps = ROWS // STEP_PAIRS
    lengths_copy = pltpu.make_async_copy(lengths_hbm, lengths_ref, sems.at[2 * steps])
    lengths_copy.start()
    for n in range(steps):
        for copy in copies(n):
            copy.start()
    lengths_copy.wait()
    slot = lax.broadcasted_iota(jnp.int32, (WIDTH, SLOTS), 1)
    for n in range(steps):
        for copy in copies(n):
            copy.wait()
        for p in range(n * STEP_PAIRS, (n + 1) * STEP_PAIRS):
            acts = acts_ref[p]
            acts = jnp.where(slot < lengths_ref[first + p], acts, jnp.zeros_like(acts))
            wide_ref[pl.ds(p * PITCH, WIDTH), :] = lax.dot_general(
                grads_ref[p],
                jnp.concatenate([acts, acts], axis=0),
                (((1,), (1,)), ((), ())),
                preferred_element_type=F32,
            )
    low = lax.broadcasted_iota(jnp.int32, (ROWS, 128), 1) < WIDTH
    for c in range(FEATURES // 128):
        even = wide_ref[pl.ds(2 * c, ROWS, stride=PITCH), :]
        odd = wide_ref[pl.ds(2 * c + 1, ROWS, stride=PITCH), :]
        out_ref[:, c * 128 : (c + 1) * 128] = jnp.where(low, even, odd).astype(BF16)


def query_grads(lengths, activations, out_grads, chunk):
    hbm = pl.BlockSpec(memory_space=pltpu.HBM)
    return pl.pallas_call(
        functools.partial(grad_kernel, chunk * ROWS),
        out_shape=jax.ShapeDtypeStruct((ROWS, FEATURES), BF16),
        in_specs=[hbm] * 3,
        scratch_shapes=[
            pltpu.VMEM((ROWS, WIDTH, SLOTS), BF16),
            pltpu.VMEM((ROWS, WIDTH, SLOTS), BF16),
            pltpu.SMEM((PAIRS,), jnp.int32),
            pltpu.VMEM((ROWS * PITCH, 128), F32),
            pltpu.SemaphoreType.DMA((2 * (ROWS // STEP_PAIRS) + 1,)),
        ],
        compiler_params=pltpu.CompilerParams(vmem_limit_bytes=16 << 20),
        name="query_grads",
    )(lengths, activations, out_grads)


def score_kernel(*refs):
    blocks, (mine_ref, other_ref), outs = refs[:8], refs[8:10], refs[10:14]
    rows_ref, sem = refs[14:]
    step = pl.program_id(0)
    x, _, y, z_hi, core = place()

    @pl.when(step == 0)
    def _():
        copies = [
            pltpu.make_async_copy(block, rows_ref.at[pl.ds(i * ROWS, ROWS)], sem.at[i])
            for i, block in enumerate(blocks)
        ]
        for copy in copies:
            copy.start()
        for copy in copies:
            copy.wait()

    def part(weights_ref, rel_core, tile):
        got = lax.dot_general(
            rows_ref[...],
            weights_ref[...],
            (((1,), (1,)), ((), ())),
            preferred_element_type=F32,
        ).astype(BF16)
        for rel_z in range(2):
            to_x = 2 * ((z_hi + rel_z) % 2) + core
            away = (to_x - x + 4) % 4
            if rel_core == 0:
                buf = jnp.where(away == 0, 1, jnp.where(away == 1, 3, jnp.where(away == 2, 2, 0)))
            else:
                buf = jnp.where(away == 0, 0, jnp.where(away == 1, 2, jnp.where(away == 2, 3, 1)))
            for b in range(4):

                @pl.when(buf == b)
                def _():
                    for j, dy in enumerate((0, 3, 1, 2)):
                        row = pl.multiple_of(((y + dy) % 4) * ROWS, ROWS)
                        at = (rel_z * 4 + j) * ROWS
                        outs[b][pl.ds(row, ROWS), tile * COLS : (tile + 1) * COLS] = got[at : at + ROWS]

    tiles = HELD // COLS
    for s in range(2 * tiles):

        @pl.when(step == s)
        def _():
            part(mine_ref if s < tiles else other_ref, s // tiles, s % tiles)


def partial_scores(blocks, mine, other):
    tiles = HELD // COLS
    out = pl.BlockSpec((4 * ROWS, HELD), lambda i: (0, 0))
    return pl.pallas_call(
        score_kernel,
        out_shape=[jax.ShapeDtypeStruct((4 * ROWS, HELD), BF16)] * 4,
        grid=(2 * tiles,),
        in_specs=[pl.BlockSpec(memory_space=pl.ANY)] * 8
        + [
            pl.BlockSpec((COLS, FEATURES), lambda i: (jnp.minimum(i, tiles - 1), 0)),
            pl.BlockSpec((COLS, FEATURES), lambda i: (jnp.maximum(i - tiles, 0), 0)),
        ],
        out_specs=[out] * 4,
        scratch_shapes=[
            pltpu.VMEM((8 * ROWS, FEATURES), BF16),
            pltpu.SemaphoreType.DMA((8,)),
        ],
        compiler_params=pltpu.CompilerParams(vmem_limit_bytes=18 << 20),
        cost_estimate=pl.CostEstimate(flops=1, bytes_accessed=1, transcendentals=0),
        name="partial_scores",
    )(*blocks, mine, other)


def cross_sum_kernel(b_ref, c_ref, a_ref, d_ref, own_ref, keep_ref, *outs):
    x, z_lo, _, _, core = place()
    match = (x % 2) == core
    for k in range(4):
        rows = pl.ds(pl.multiple_of(((z_lo + k) % 4) * ROWS, ROWS), ROWS)
        near = own_ref[rows, :].astype(F32) + b_ref[rows, :].astype(F32)
        last = jnp.where(match, near, d_ref[rows, :].astype(F32))
        total = (a_ref[rows, :].astype(F32) + c_ref[rows, :].astype(F32)) + last
        if k == 0:
            keep_ref[...] = total
        else:
            outs[k - 1][...] = total.astype(BF16)


def cross_sum(*parts):
    return pl.pallas_call(
        cross_sum_kernel,
        out_shape=[jax.ShapeDtypeStruct((ROWS, HELD), F32)]
        + [jax.ShapeDtypeStruct((ROWS, HELD), BF16)] * 3,
        compiler_params=pltpu.CompilerParams(vmem_limit_bytes=16 << 20),
        name="cross_sum",
    )(*parts)


def final_kernel(*refs):
    pick_ref, out_ref = refs[-2:]
    totals = []
    for n in range(CHUNKS):
        keep, first, second, third = refs[4 * n : 4 * n + 4]
        total = keep[...] + first[...].astype(F32)
        totals.append(total + (second[...].astype(F32) + third[...].astype(F32)))
    total = jnp.concatenate(totals, axis=0)
    high = total.astype(BF16)
    rest = total - high.astype(F32)
    middle = rest.astype(BF16)
    low = (rest - middle.astype(F32)).astype(BF16)
    picked = lax.dot_general(
        jnp.concatenate([high, middle, low], axis=0),
        pick_ref[...],
        (((1,), (0,)), ((), ())),
        preferred_element_type=F32,
    )
    out_ref[...] = picked[:PAIRS] + (picked[PAIRS : 2 * PAIRS] + picked[2 * PAIRS :])


def final_sum(parts, pick):
    return pl.pallas_call(
        final_kernel,
        out_shape=jax.ShapeDtypeStruct((PAIRS, HELD), F32),
        compiler_params=pltpu.CompilerParams(vmem_limit_bytes=16 << 20),
        name="final_sum",
    )(*parts, pick)


def store_pairs(move):
    pairs = []
    for z_lo in range(4):
        for x in range(4):
            pairs.append((node(x, z_lo, 0, 0, 0)[0], node(*move(x, z_lo), 0, 0, 0)[0]))
    return pairs


def all_pairs(move):
    pairs = []
    for z_lo in range(4):
        for x in range(4):
            for y in range(4):
                for z_hi in range(2):
                    for core in range(2):
                        dst = move(x, core)
                        if dst is None:
                            continue
                        s, g = node(x, z_lo, y, z_hi, core)
                        t, h = node(dst[0], z_lo, y, z_hi, dst[1])
                        pairs.append((s * 16 + g, t * 16 + h))
    return pairs


def along(value, move):
    return lax.ppermute(value, "group", group_pairs(move))


def fence_kernel(*refs):
    pass


def after(values, *others):
    hold = pl.BlockSpec(memory_space=pl.ANY)
    return pl.pallas_call(
        fence_kernel,
        out_shape=[jax.ShapeDtypeStruct(v.shape, v.dtype) for v in values],
        in_specs=[hold] * (len(values) + len(others)),
        out_specs=[hold] * len(values),
        input_output_aliases={i: i for i in range(len(values))},
        compiler_params=pltpu.CompilerParams(vmem_limit_bytes=1 << 20),
        name="fence",
    )(*values, *others)


def up(value):
    return along(value, lambda y, z, c: (y + 1, z, c))


def down(value):
    return along(value, lambda y, z, c: (y - 1, z, c))


def beyond(value):
    return along(value, lambda y, z, c: (y, z + 1, c))


def first_scores(a, b, stored, other):
    far_a = beyond(a)
    a_below, a_above = up(a), down(a)
    (b,) = after((b,), other)
    far_b = beyond(b)
    b_below, b_above = up(b), down(b)
    far_a, a_below, a_above = after((far_a, a_below, a_above), b_below, b_above)
    a_opposite = up(a_below)
    far_a_above, far_a_below = down(far_a), up(far_a)
    far_a_opposite = down(far_a_above)
    far_b, b_below = after((far_b, b_below), far_a_above, far_a_below)
    b_opposite = up(b_below)
    far_b_above, far_b_below = down(far_b), up(far_b)
    a_blocks = [a, a_below, a_above, a_opposite, far_a, far_a_below, far_a_above, far_a_opposite]
    a_bufs = list(partial_scores(a_blocks, stored, other))
    (far_b_above,) = after((far_b_above,), a_bufs[1])
    far_b_opposite = down(far_b_above)
    b_blocks = [b, b_below, b_above, b_opposite, far_b, far_b_below, far_b_above, far_b_opposite]
    return a_bufs, b_blocks


def join_kernel(send_ref, got_ref, out_ref):
    x, _, _, _, core = place()
    got = jnp.where((x % 2) == core, 0.0, got_ref[...].astype(F32))
    out_ref[...] = (send_ref[...].astype(F32) + got).astype(BF16)


def join(send, got):
    return pl.pallas_call(
        join_kernel,
        out_shape=jax.ShapeDtypeStruct(send.shape, BF16),
        compiler_params=pltpu.CompilerParams(vmem_limit_bytes=16 << 20),
        name="join",
    )(send, got)


def over_x(bufs):
    def send(value, move):
        return lax.ppermute(value, ("store", "group"), all_pairs(move))

    def match(x, core):
        return x % 2 == core

    got_b = send(bufs[3], lambda x, c: (x - 1, c) if match(x, c) else (x + 1, c))
    got_c = send(bufs[0], lambda x, c: (x, 1 - c) if match(x, c) else (x - 1, c))
    got_a = send(bufs[2], lambda x, c: (x + 2, c) if match(x, c) else (x + 1, 1 - c))
    joined = join(bufs[1], got_b)
    got_d = send(joined, lambda x, c: None if match(x, c) else (x - 1, 1 - c))
    return [got_b, got_c, got_a, got_d]


def on_device(activations, out_grads, stored, lengths, store_ids):
    stored = stored.reshape(HELD, FEATURES)
    other = lax.ppermute(stored, "group", group_pairs(lambda y, z, c: (y, z, 1 - c)))
    pick = (store_ids[None, :] == jnp.arange(HELD, dtype=jnp.int32)[:, None]).astype(BF16)
    inputs = [
        pltpu.with_memory_space_constraint(v, pltpu.HBM) for v in (lengths, activations, out_grads)
    ]
    a, b = (query_grads(*inputs, n) for n in range(CHUNKS))
    a_bufs, b_blocks = first_scores(a, b, stored, other)
    a_got = over_x(a_bufs)
    b_bufs = list(partial_scores(b_blocks, stored, other))
    b_bufs = after(b_bufs, *a_got[:3])
    b_got = over_x(b_bufs)
    parts = []
    for got, bufs in ((a_got, a_bufs), (b_got, b_bufs)):
        keep, *sends = cross_sum(*got, bufs[1])
        parts.append(keep)
        for k, send in enumerate(sends, 1):
            parts.append(lax.ppermute(send, "store", store_pairs(lambda x, z: (x, z + k))))
    return final_sum(parts, pick)


def solution(mesh):
    in_specs = (
        P("group", "store", None, None),
        P("group", "store", None, None),
        P("group", "store", None),
        P("group"),
        P("group"),
    )
    out_specs = P("store", "group")
    return jax.shard_map(
        on_device, mesh=mesh, in_specs=in_specs, out_specs=out_specs, check_vma=False
    )
```

```python
import functools

import jax
import jax.numpy as jnp
from jax import lax
from jax.experimental import pallas as pl
from jax.experimental.pallas import tpu as pltpu
from jax.sharding import PartitionSpec as P

CHUNKS = 2
PAIRS = 64
ROWS = PAIRS // CHUNKS
WIDTH = 64
SLOTS = 256
FEATURES = WIDTH * WIDTH
HELD = 768
STEP_PAIRS = 8
PITCH = 72
COLS = 256
F32 = jnp.float32
BF16 = jnp.bfloat16


def node(x, z_lo, y, z_hi, core):
    return (z_lo % 4) * 4 + x % 4, ((y % 4) * 2 + z_hi % 2) * 2 + core % 2


def group_pairs(move):
    pairs = []
    for y in range(4):
        for z_hi in range(2):
            for core in range(2):
                dst = move(y, z_hi, core)
                if dst is not None:
                    pairs.append((node(0, 0, y, z_hi, core)[1], node(0, 0, *dst)[1]))
    return pairs


def place():
    store, group = lax.axis_index("store"), lax.axis_index("group")
    return store % 4, store // 4, group // 4, (group // 2) % 2, group % 2


def grad_kernel(first, lengths_hbm, acts_hbm, grads_hbm, out_ref, acts_ref, grads_ref, lengths_ref, wide_ref, sems):
    def copies(n):
        src, dst = pl.ds(first + n * STEP_PAIRS, STEP_PAIRS), pl.ds(n * STEP_PAIRS, STEP_PAIRS)
        return (
            pltpu.make_async_copy(acts_hbm.at[src, 0], acts_ref.at[dst], sems.at[2 * n]),
            pltpu.make_async_copy(grads_hbm.at[src, 0], grads_ref.at[dst], sems.at[2 * n + 1]),
        )

    steps = ROWS // STEP_PAIRS
    lengths_copy = pltpu.make_async_copy(lengths_hbm, lengths_ref, sems.at[2 * steps])
    lengths_copy.start()
    for n in range(steps):
        for copy in copies(n):
            copy.start()
    lengths_copy.wait()
    slot = lax.broadcasted_iota(jnp.int32, (WIDTH, SLOTS), 1)
    for n in range(steps):
        for copy in copies(n):
            copy.wait()
        for p in range(n * STEP_PAIRS, (n + 1) * STEP_PAIRS):
            acts = acts_ref[p]
            acts = jnp.where(slot < lengths_ref[first + p], acts, jnp.zeros_like(acts))
            wide_ref[pl.ds(p * PITCH, WIDTH), :] = lax.dot_general(
                grads_ref[p],
                jnp.concatenate([acts, acts], axis=0),
                (((1,), (1,)), ((), ())),
                preferred_element_type=F32,
            )
    low = lax.broadcasted_iota(jnp.int32, (ROWS, 128), 1) < WIDTH
    for c in range(FEATURES // 128):
        even = wide_ref[pl.ds(2 * c, ROWS, stride=PITCH), :]
        odd = wide_ref[pl.ds(2 * c + 1, ROWS, stride=PITCH), :]
        out_ref[:, c * 128 : (c + 1) * 128] = jnp.where(low, even, odd).astype(BF16)


def query_grads(lengths, activations, out_grads, chunk):
    hbm = pl.BlockSpec(memory_space=pltpu.HBM)
    return pl.pallas_call(
        functools.partial(grad_kernel, chunk * ROWS),
        out_shape=jax.ShapeDtypeStruct((ROWS, FEATURES), BF16),
        in_specs=[hbm] * 3,
        scratch_shapes=[
            pltpu.VMEM((ROWS, WIDTH, SLOTS), BF16),
            pltpu.VMEM((ROWS, WIDTH, SLOTS), BF16),
            pltpu.SMEM((PAIRS,), jnp.int32),
            pltpu.VMEM((ROWS * PITCH, 128), F32),
            pltpu.SemaphoreType.DMA((2 * (ROWS // STEP_PAIRS) + 1,)),
        ],
        compiler_params=pltpu.CompilerParams(vmem_limit_bytes=16 << 20),
        name="query_grads",
    )(lengths, activations, out_grads)


def score_kernel(*refs):
    blocks, (mine_ref, other_ref), outs = refs[:8], refs[8:10], refs[10:14]
    rows_ref, sem = refs[14:]
    step = pl.program_id(0)
    x, _, y, z_hi, core = place()

    @pl.when(step == 0)
    def _():
        copies = [
            pltpu.make_async_copy(block, rows_ref.at[pl.ds(i * ROWS, ROWS)], sem.at[i])
            for i, block in enumerate(blocks)
        ]
        for copy in copies:
            copy.start()
        for copy in copies:
            copy.wait()

    def part(weights_ref, rel_core, tile):
        got = lax.dot_general(
            rows_ref[...],
            weights_ref[...],
            (((1,), (1,)), ((), ())),
            preferred_element_type=F32,
        ).astype(BF16)
        for rel_z in range(2):
            to_x = 2 * ((z_hi + rel_z) % 2) + core
            away = (to_x - x + 4) % 4
            if rel_core == 0:
                buf = jnp.where(away == 0, 1, jnp.where(away == 1, 3, jnp.where(away == 2, 2, 0)))
            else:
                buf = jnp.where(away == 0, 0, jnp.where(away == 1, 2, jnp.where(away == 2, 3, 1)))
            for b in range(4):

                @pl.when(buf == b)
                def _():
                    for j, dy in enumerate((0, 3, 1, 2)):
                        row = pl.multiple_of(((y + dy) % 4) * ROWS, ROWS)
                        at = (rel_z * 4 + j) * ROWS
                        outs[b][pl.ds(row, ROWS), tile * COLS : (tile + 1) * COLS] = got[at : at + ROWS]

    tiles = HELD // COLS
    for s in range(2 * tiles):

        @pl.when(step == s)
        def _():
            part(mine_ref if s < tiles else other_ref, s // tiles, s % tiles)


def partial_scores(blocks, mine, other):
    tiles = HELD // COLS
    out = pl.BlockSpec((4 * ROWS, HELD), lambda i: (0, 0))
    return pl.pallas_call(
        score_kernel,
        out_shape=[jax.ShapeDtypeStruct((4 * ROWS, HELD), BF16)] * 4,
        grid=(2 * tiles,),
        in_specs=[pl.BlockSpec(memory_space=pl.ANY)] * 8
        + [
            pl.BlockSpec((COLS, FEATURES), lambda i: (jnp.minimum(i, tiles - 1), 0)),
            pl.BlockSpec((COLS, FEATURES), lambda i: (jnp.maximum(i - tiles, 0), 0)),
        ],
        out_specs=[out] * 4,
        scratch_shapes=[
            pltpu.VMEM((8 * ROWS, FEATURES), BF16),
            pltpu.SemaphoreType.DMA((8,)),
        ],
        compiler_params=pltpu.CompilerParams(vmem_limit_bytes=18 << 20),
        cost_estimate=pl.CostEstimate(flops=1, bytes_accessed=1, transcendentals=0),
        name="partial_scores",
    )(*blocks, mine, other)


def cross_sum_kernel(b_ref, c_ref, a_ref, d_ref, own_ref, keep_ref, *outs):
    x, z_lo, _, _, core = place()
    match = (x % 2) == core
    for k in range(4):
        rows = pl.ds(pl.multiple_of(((z_lo + k) % 4) * ROWS, ROWS), ROWS)
        near = own_ref[rows, :].astype(F32) + b_ref[rows, :].astype(F32)
        last = jnp.where(match, near, d_ref[rows, :].astype(F32))
        total = (a_ref[rows, :].astype(F32) + c_ref[rows, :].astype(F32)) + last
        if k == 0:
            keep_ref[...] = total
        else:
            outs[k - 1][...] = total.astype(BF16)


def cross_sum(*parts):
    return pl.pallas_call(
        cross_sum_kernel,
        out_shape=[jax.ShapeDtypeStruct((ROWS, HELD), F32)]
        + [jax.ShapeDtypeStruct((ROWS, HELD), BF16)] * 3,
        compiler_params=pltpu.CompilerParams(vmem_limit_bytes=16 << 20),
        name="cross_sum",
    )(*parts)


def final_kernel(*refs):
    pick_ref, out_ref = refs[-2:]
    totals = []
    for n in range(CHUNKS):
        keep, first, second, third = refs[4 * n : 4 * n + 4]
        total = keep[...] + first[...].astype(F32)
        totals.append(total + (second[...].astype(F32) + third[...].astype(F32)))
    total = jnp.concatenate(totals, axis=0)
    high = total.astype(BF16)
    rest = total - high.astype(F32)
    middle = rest.astype(BF16)
    low = (rest - middle.astype(F32)).astype(BF16)
    picked = lax.dot_general(
        jnp.concatenate([high, middle, low], axis=0),
        pick_ref[...],
        (((1,), (0,)), ((), ())),
        preferred_element_type=F32,
    )
    out_ref[...] = picked[:PAIRS] + (picked[PAIRS : 2 * PAIRS] + picked[2 * PAIRS :])


def final_sum(parts, pick):
    return pl.pallas_call(
        final_kernel,
        out_shape=jax.ShapeDtypeStruct((PAIRS, HELD), F32),
        compiler_params=pltpu.CompilerParams(vmem_limit_bytes=16 << 20),
        name="final_sum",
    )(*parts, pick)


def store_pairs(move):
    pairs = []
    for z_lo in range(4):
        for x in range(4):
            pairs.append((node(x, z_lo, 0, 0, 0)[0], node(*move(x, z_lo), 0, 0, 0)[0]))
    return pairs


def all_pairs(move):
    pairs = []
    for z_lo in range(4):
        for x in range(4):
            for y in range(4):
                for z_hi in range(2):
                    for core in range(2):
                        dst = move(x, core)
                        if dst is None:
                            continue
                        s, g = node(x, z_lo, y, z_hi, core)
                        t, h = node(dst[0], z_lo, y, z_hi, dst[1])
                        pairs.append((s * 16 + g, t * 16 + h))
    return pairs


def along(value, move):
    return lax.ppermute(value, "group", group_pairs(move))


def fence_kernel(*refs):
    pass


def after(values, *others):
    hold = pl.BlockSpec(memory_space=pl.ANY)
    return pl.pallas_call(
        fence_kernel,
        out_shape=[jax.ShapeDtypeStruct(v.shape, v.dtype) for v in values],
        in_specs=[hold] * (len(values) + len(others)),
        out_specs=[hold] * len(values),
        input_output_aliases={i: i for i in range(len(values))},
        compiler_params=pltpu.CompilerParams(vmem_limit_bytes=1 << 20),
        name="fence",
    )(*values, *others)


def up(value):
    return along(value, lambda y, z, c: (y + 1, z, c))


def down(value):
    return along(value, lambda y, z, c: (y - 1, z, c))


def beyond(value):
    return along(value, lambda y, z, c: (y, z + 1, c))


def first_scores(a, b, stored, other):
    far_a = beyond(a)
    a_below, a_above = up(a), down(a)
    (b,) = after((b,), other)
    far_b = beyond(b)
    b_below, b_above = up(b), down(b)
    a_opposite = up(a_below)
    far_a, a_above = after((far_a, a_above), a_opposite, b_above)
    far_a_above, far_a_below = down(far_a), up(far_a)
    far_a_opposite = down(far_a_above)
    far_b, b_below = after((far_b, b_below), far_a_above, far_a_below)
    b_opposite = up(b_below)
    far_b_above, far_b_below = down(far_b), up(far_b)
    a_blocks = [a, a_below, a_above, a_opposite, far_a, far_a_below, far_a_above, far_a_opposite]
    a_bufs = list(partial_scores(a_blocks, stored, other))
    (far_b_above,) = after((far_b_above,), a_bufs[1])
    far_b_opposite = down(far_b_above)
    b_blocks = [b, b_below, b_above, b_opposite, far_b, far_b_below, far_b_above, far_b_opposite]
    return a_bufs, b_blocks


def join_kernel(send_ref, got_ref, out_ref):
    x, _, _, _, core = place()
    got = jnp.where((x % 2) == core, 0.0, got_ref[...].astype(F32))
    out_ref[...] = (send_ref[...].astype(F32) + got).astype(BF16)


def join(send, got):
    return pl.pallas_call(
        join_kernel,
        out_shape=jax.ShapeDtypeStruct(send.shape, BF16),
        compiler_params=pltpu.CompilerParams(vmem_limit_bytes=16 << 20),
        name="join",
    )(send, got)


def over_x(bufs):
    def send(value, move):
        return lax.ppermute(value, ("store", "group"), all_pairs(move))

    def match(x, core):
        return x % 2 == core

    got_b = send(bufs[3], lambda x, c: (x - 1, c) if match(x, c) else (x + 1, c))
    got_c = send(bufs[0], lambda x, c: (x, 1 - c) if match(x, c) else (x - 1, c))
    got_a = send(bufs[2], lambda x, c: (x + 2, c) if match(x, c) else (x + 1, 1 - c))
    joined = join(bufs[1], got_b)
    got_d = send(joined, lambda x, c: None if match(x, c) else (x - 1, 1 - c))
    return [got_b, got_c, got_a, got_d]


def on_device(activations, out_grads, stored, lengths, store_ids):
    stored = stored.reshape(HELD, FEATURES)
    other = lax.ppermute(stored, "group", group_pairs(lambda y, z, c: (y, z, 1 - c)))
    pick = (store_ids[None, :] == jnp.arange(HELD, dtype=jnp.int32)[:, None]).astype(BF16)
    inputs = [
        pltpu.with_memory_space_constraint(v, pltpu.HBM) for v in (lengths, activations, out_grads)
    ]
    a, b = (query_grads(*inputs, n) for n in range(CHUNKS))
    a_bufs, b_blocks = first_scores(a, b, stored, other)
    a_got = over_x(a_bufs)
    b_bufs = list(partial_scores(b_blocks, stored, other))
    b_bufs = after(b_bufs, *a_got[:3])
    b_got = over_x(b_bufs)
    parts = []
    for got, bufs in ((a_got, a_bufs), (b_got, b_bufs)):
        keep, *sends = cross_sum(*got, bufs[1])
        parts.append(keep)
        for k, send in enumerate(sends, 1):
            parts.append(lax.ppermute(send, "store", store_pairs(lambda x, z: (x, z + k))))
    return final_sum(parts, pick)


def solution(mesh):
    in_specs = (
        P("group", "store", None, None),
        P("group", "store", None, None),
        P("group", "store", None),
        P("group"),
        P("group"),
    )
    out_specs = P("store", "group")
    return jax.shard_map(
        on_device, mesh=mesh, in_specs=in_specs, out_specs=out_specs, check_vma=False
    )
```

```python
import functools

import jax
import jax.numpy as jnp
from jax import lax
from jax.experimental import pallas as pl
from jax.experimental.pallas import tpu as pltpu
from jax.sharding import PartitionSpec as P

CHUNKS = 2
PAIRS = 64
ROWS = PAIRS // CHUNKS
WIDTH = 64
SLOTS = 256
FEATURES = WIDTH * WIDTH
HELD = 768
STEP_PAIRS = 8
PITCH = 72
COLS = 256
F32 = jnp.float32
BF16 = jnp.bfloat16


def node(x, z_lo, y, z_hi, core):
    return (z_lo % 4) * 4 + x % 4, ((y % 4) * 2 + z_hi % 2) * 2 + core % 2


def group_pairs(move):
    pairs = []
    for y in range(4):
        for z_hi in range(2):
            for core in range(2):
                dst = move(y, z_hi, core)
                if dst is not None:
                    pairs.append((node(0, 0, y, z_hi, core)[1], node(0, 0, *dst)[1]))
    return pairs


def place():
    store, group = lax.axis_index("store"), lax.axis_index("group")
    return store % 4, store // 4, group // 4, (group // 2) % 2, group % 2


def grad_kernel(first, lengths_hbm, acts_hbm, grads_hbm, out_ref, acts_ref, grads_ref, lengths_ref, wide_ref, sems):
    def copies(n):
        src, dst = pl.ds(first + n * STEP_PAIRS, STEP_PAIRS), pl.ds(n * STEP_PAIRS, STEP_PAIRS)
        return (
            pltpu.make_async_copy(acts_hbm.at[src, 0], acts_ref.at[dst], sems.at[2 * n]),
            pltpu.make_async_copy(grads_hbm.at[src, 0], grads_ref.at[dst], sems.at[2 * n + 1]),
        )

    steps = ROWS // STEP_PAIRS
    lengths_copy = pltpu.make_async_copy(lengths_hbm, lengths_ref, sems.at[2 * steps])
    lengths_copy.start()
    for n in range(steps):
        for copy in copies(n):
            copy.start()
    lengths_copy.wait()
    slot = lax.broadcasted_iota(jnp.int32, (WIDTH, SLOTS), 1)
    for n in range(steps):
        for copy in copies(n):
            copy.wait()
        for p in range(n * STEP_PAIRS, (n + 1) * STEP_PAIRS):
            acts = acts_ref[p]
            acts = jnp.where(slot < lengths_ref[first + p], acts, jnp.zeros_like(acts))
            wide_ref[pl.ds(p * PITCH, WIDTH), :] = lax.dot_general(
                grads_ref[p],
                jnp.concatenate([acts, acts], axis=0),
                (((1,), (1,)), ((), ())),
                preferred_element_type=F32,
            )
    low = lax.broadcasted_iota(jnp.int32, (ROWS, 128), 1) < WIDTH
    for c in range(FEATURES // 128):
        even = wide_ref[pl.ds(2 * c, ROWS, stride=PITCH), :]
        odd = wide_ref[pl.ds(2 * c + 1, ROWS, stride=PITCH), :]
        out_ref[:, c * 128 : (c + 1) * 128] = jnp.where(low, even, odd).astype(BF16)


def query_grads(lengths, activations, out_grads, chunk):
    hbm = pl.BlockSpec(memory_space=pltpu.HBM)
    return pl.pallas_call(
        functools.partial(grad_kernel, chunk * ROWS),
        out_shape=jax.ShapeDtypeStruct((ROWS, FEATURES), BF16),
        in_specs=[hbm] * 3,
        scratch_shapes=[
            pltpu.VMEM((ROWS, WIDTH, SLOTS), BF16),
            pltpu.VMEM((ROWS, WIDTH, SLOTS), BF16),
            pltpu.SMEM((PAIRS,), jnp.int32),
            pltpu.VMEM((ROWS * PITCH, 128), F32),
            pltpu.SemaphoreType.DMA((2 * (ROWS // STEP_PAIRS) + 1,)),
        ],
        compiler_params=pltpu.CompilerParams(vmem_limit_bytes=16 << 20),
        name="query_grads",
    )(lengths, activations, out_grads)


def score_kernel(*refs):
    blocks, (mine_ref, other_ref), outs = refs[:8], refs[8:10], refs[10:14]
    rows_ref, sem = refs[14:]
    step = pl.program_id(0)
    x, _, y, z_hi, core = place()

    @pl.when(step == 0)
    def _():
        copies = [
            pltpu.make_async_copy(block, rows_ref.at[pl.ds(i * ROWS, ROWS)], sem.at[i])
            for i, block in enumerate(blocks)
        ]
        for copy in copies:
            copy.start()
        for copy in copies:
            copy.wait()

    def part(weights_ref, rel_core, tile):
        got = lax.dot_general(
            rows_ref[...],
            weights_ref[...],
            (((1,), (1,)), ((), ())),
            preferred_element_type=F32,
        ).astype(BF16)
        for rel_z in range(2):
            to_x = 2 * ((z_hi + rel_z) % 2) + core
            away = (to_x - x + 4) % 4
            if rel_core == 0:
                buf = jnp.where(away == 0, 1, jnp.where(away == 1, 3, jnp.where(away == 2, 2, 0)))
            else:
                buf = jnp.where(away == 0, 0, jnp.where(away == 1, 2, jnp.where(away == 2, 3, 1)))
            for b in range(4):

                @pl.when(buf == b)
                def _():
                    for j, dy in enumerate((0, 3, 1, 2)):
                        row = pl.multiple_of(((y + dy) % 4) * ROWS, ROWS)
                        at = (rel_z * 4 + j) * ROWS
                        outs[b][pl.ds(row, ROWS), tile * COLS : (tile + 1) * COLS] = got[at : at + ROWS]

    tiles = HELD // COLS
    for s in range(2 * tiles):

        @pl.when(step == s)
        def _():
            part(mine_ref if s < tiles else other_ref, s // tiles, s % tiles)


def partial_scores(blocks, mine, other):
    tiles = HELD // COLS
    out = pl.BlockSpec((4 * ROWS, HELD), lambda i: (0, 0))
    return pl.pallas_call(
        score_kernel,
        out_shape=[jax.ShapeDtypeStruct((4 * ROWS, HELD), BF16)] * 4,
        grid=(2 * tiles,),
        in_specs=[pl.BlockSpec(memory_space=pl.ANY)] * 8
        + [
            pl.BlockSpec((COLS, FEATURES), lambda i: (jnp.minimum(i, tiles - 1), 0)),
            pl.BlockSpec((COLS, FEATURES), lambda i: (jnp.maximum(i - tiles, 0), 0)),
        ],
        out_specs=[out] * 4,
        scratch_shapes=[
            pltpu.VMEM((8 * ROWS, FEATURES), BF16),
            pltpu.SemaphoreType.DMA((8,)),
        ],
        compiler_params=pltpu.CompilerParams(vmem_limit_bytes=18 << 20),
        cost_estimate=pl.CostEstimate(flops=1, bytes_accessed=1, transcendentals=0),
        name="partial_scores",
    )(*blocks, mine, other)


def cross_sum_kernel(b_ref, c_ref, a_ref, d_ref, own_ref, keep_ref, *outs):
    x, z_lo, _, _, core = place()
    match = (x % 2) == core
    for k in range(4):
        rows = pl.ds(pl.multiple_of(((z_lo + k) % 4) * ROWS, ROWS), ROWS)
        near = own_ref[rows, :].astype(F32) + b_ref[rows, :].astype(F32)
        last = jnp.where(match, near, d_ref[rows, :].astype(F32))
        total = (a_ref[rows, :].astype(F32) + c_ref[rows, :].astype(F32)) + last
        if k == 0:
            keep_ref[...] = total
        else:
            outs[k - 1][...] = total.astype(BF16)


def cross_sum(*parts):
    return pl.pallas_call(
        cross_sum_kernel,
        out_shape=[jax.ShapeDtypeStruct((ROWS, HELD), F32)]
        + [jax.ShapeDtypeStruct((ROWS, HELD), BF16)] * 3,
        compiler_params=pltpu.CompilerParams(vmem_limit_bytes=16 << 20),
        name="cross_sum",
    )(*parts)


def final_kernel(*refs):
    pick_ref, out_ref = refs[-2:]
    totals = []
    for n in range(CHUNKS):
        keep, first, second, third = refs[4 * n : 4 * n + 4]
        total = keep[...] + first[...].astype(F32)
        totals.append(total + (second[...].astype(F32) + third[...].astype(F32)))
    total = jnp.concatenate(totals, axis=0)
    high = total.astype(BF16)
    rest = total - high.astype(F32)
    middle = rest.astype(BF16)
    low = (rest - middle.astype(F32)).astype(BF16)
    picked = lax.dot_general(
        jnp.concatenate([high, middle, low], axis=0),
        pick_ref[...],
        (((1,), (0,)), ((), ())),
        preferred_element_type=F32,
    )
    out_ref[...] = picked[:PAIRS] + (picked[PAIRS : 2 * PAIRS] + picked[2 * PAIRS :])


def final_sum(parts, pick):
    return pl.pallas_call(
        final_kernel,
        out_shape=jax.ShapeDtypeStruct((PAIRS, HELD), F32),
        compiler_params=pltpu.CompilerParams(vmem_limit_bytes=16 << 20),
        name="final_sum",
    )(*parts, pick)


def store_pairs(move):
    pairs = []
    for z_lo in range(4):
        for x in range(4):
            pairs.append((node(x, z_lo, 0, 0, 0)[0], node(*move(x, z_lo), 0, 0, 0)[0]))
    return pairs


def all_pairs(move):
    pairs = []
    for z_lo in range(4):
        for x in range(4):
            for y in range(4):
                for z_hi in range(2):
                    for core in range(2):
                        dst = move(x, core)
                        if dst is None:
                            continue
                        s, g = node(x, z_lo, y, z_hi, core)
                        t, h = node(dst[0], z_lo, y, z_hi, dst[1])
                        pairs.append((s * 16 + g, t * 16 + h))
    return pairs


def along(value, move):
    return lax.ppermute(value, "group", group_pairs(move))


def fence_kernel(*refs):
    pass


def after(values, *others):
    hold = pl.BlockSpec(memory_space=pl.ANY)
    return pl.pallas_call(
        fence_kernel,
        out_shape=[jax.ShapeDtypeStruct(v.shape, v.dtype) for v in values],
        in_specs=[hold] * (len(values) + len(others)),
        out_specs=[hold] * len(values),
        input_output_aliases={i: i for i in range(len(values))},
        compiler_params=pltpu.CompilerParams(vmem_limit_bytes=1 << 20),
        name="fence",
    )(*values, *others)


def up(value):
    return along(value, lambda y, z, c: (y + 1, z, c))


def down(value):
    return along(value, lambda y, z, c: (y - 1, z, c))


def beyond(value):
    return along(value, lambda y, z, c: (y, z + 1, c))


def first_scores(a, b, stored, other):
    far_a = beyond(a)
    a_below, a_above = up(a), down(a)
    (b,) = after((b,), other)
    far_b = beyond(b)
    b_below, b_above = up(b), down(b)
    a_opposite = up(a_below)
    far_a, a_above = after((far_a, a_above), b_below, b_above)
    far_a_above = down(far_a)
    (far_a,) = after((far_a,), a_opposite)
    far_a_below = up(far_a)
    far_a_opposite = down(far_a_above)
    far_b, b_below = after((far_b, b_below), far_a_above, far_a_below)
    b_opposite = up(b_below)
    far_b_above, far_b_below = down(far_b), up(far_b)
    a_blocks = [a, a_below, a_above, a_opposite, far_a, far_a_below, far_a_above, far_a_opposite]
    a_bufs = list(partial_scores(a_blocks, stored, other))
    (far_b_above,) = after((far_b_above,), a_bufs[1])
    far_b_opposite = down(far_b_above)
    b_blocks = [b, b_below, b_above, b_opposite, far_b, far_b_below, far_b_above, far_b_opposite]
    return a_bufs, b_blocks


def join_kernel(send_ref, got_ref, out_ref):
    x, _, _, _, core = place()
    got = jnp.where((x % 2) == core, 0.0, got_ref[...].astype(F32))
    out_ref[...] = (send_ref[...].astype(F32) + got).astype(BF16)


def join(send, got):
    return pl.pallas_call(
        join_kernel,
        out_shape=jax.ShapeDtypeStruct(send.shape, BF16),
        compiler_params=pltpu.CompilerParams(vmem_limit_bytes=16 << 20),
        name="join",
    )(send, got)


def over_x(bufs):
    def send(value, move):
        return lax.ppermute(value, ("store", "group"), all_pairs(move))

    def match(x, core):
        return x % 2 == core

    got_b = send(bufs[3], lambda x, c: (x - 1, c) if match(x, c) else (x + 1, c))
    got_c = send(bufs[0], lambda x, c: (x, 1 - c) if match(x, c) else (x - 1, c))
    got_a = send(bufs[2], lambda x, c: (x + 2, c) if match(x, c) else (x + 1, 1 - c))
    joined = join(bufs[1], got_b)
    got_d = send(joined, lambda x, c: None if match(x, c) else (x - 1, 1 - c))
    return [got_b, got_c, got_a, got_d]


def on_device(activations, out_grads, stored, lengths, store_ids):
    stored = stored.reshape(HELD, FEATURES)
    other = lax.ppermute(stored, "group", group_pairs(lambda y, z, c: (y, z, 1 - c)))
    pick = (store_ids[None, :] == jnp.arange(HELD, dtype=jnp.int32)[:, None]).astype(BF16)
    inputs = [
        pltpu.with_memory_space_constraint(v, pltpu.HBM) for v in (lengths, activations, out_grads)
    ]
    a, b = (query_grads(*inputs, n) for n in range(CHUNKS))
    a_bufs, b_blocks = first_scores(a, b, stored, other)
    a_got = over_x(a_bufs)
    b_bufs = list(partial_scores(b_blocks, stored, other))
    b_bufs = after(b_bufs, *a_got[:3])
    b_got = over_x(b_bufs)
    parts = []
    for got, bufs in ((a_got, a_bufs), (b_got, b_bufs)):
        keep, *sends = cross_sum(*got, bufs[1])
        parts.append(keep)
        for k, send in enumerate(sends, 1):
            parts.append(lax.ppermute(send, "store", store_pairs(lambda x, z: (x, z + k))))
    return final_sum(parts, pick)


def solution(mesh):
    in_specs = (
        P("group", "store", None, None),
        P("group", "store", None, None),
        P("group", "store", None),
        P("group"),
        P("group"),
    )
    out_specs = P("store", "group")
    return jax.shard_map(
        on_device, mesh=mesh, in_specs=in_specs, out_specs=out_specs, check_vma=False
    )
```

```python
import functools

import jax
import jax.numpy as jnp
from jax import lax
from jax.experimental import pallas as pl
from jax.experimental.pallas import tpu as pltpu
from jax.sharding import PartitionSpec as P

CHUNKS = 2
PAIRS = 64
ROWS = PAIRS // CHUNKS
WIDTH = 64
SLOTS = 256
FEATURES = WIDTH * WIDTH
HELD = 768
STEP_PAIRS = 8
PITCH = 72
COLS = 256
F32 = jnp.float32
BF16 = jnp.bfloat16


def node(x, z_lo, y, z_hi, core):
    return (z_lo % 4) * 4 + x % 4, ((y % 4) * 2 + z_hi % 2) * 2 + core % 2


def group_pairs(move):
    pairs = []
    for y in range(4):
        for z_hi in range(2):
            for core in range(2):
                dst = move(y, z_hi, core)
                if dst is not None:
                    pairs.append((node(0, 0, y, z_hi, core)[1], node(0, 0, *dst)[1]))
    return pairs


def place():
    store, group = lax.axis_index("store"), lax.axis_index("group")
    return store % 4, store // 4, group // 4, (group // 2) % 2, group % 2


def grad_kernel(first, lengths_hbm, acts_hbm, grads_hbm, out_ref, acts_ref, grads_ref, lengths_ref, wide_ref, sems):
    def copies(n):
        src, dst = pl.ds(first + n * STEP_PAIRS, STEP_PAIRS), pl.ds(n * STEP_PAIRS, STEP_PAIRS)
        return (
            pltpu.make_async_copy(acts_hbm.at[src, 0], acts_ref.at[dst], sems.at[2 * n]),
            pltpu.make_async_copy(grads_hbm.at[src, 0], grads_ref.at[dst], sems.at[2 * n + 1]),
        )

    steps = ROWS // STEP_PAIRS
    lengths_copy = pltpu.make_async_copy(lengths_hbm, lengths_ref, sems.at[2 * steps])
    lengths_copy.start()
    for n in range(steps):
        for copy in copies(n):
            copy.start()
    lengths_copy.wait()
    slot = lax.broadcasted_iota(jnp.int32, (WIDTH, SLOTS), 1)
    for n in range(steps):
        for copy in copies(n):
            copy.wait()
        for p in range(n * STEP_PAIRS, (n + 1) * STEP_PAIRS):
            acts = acts_ref[p]
            acts = jnp.where(slot < lengths_ref[first + p], acts, jnp.zeros_like(acts))
            wide_ref[pl.ds(p * PITCH, WIDTH), :] = lax.dot_general(
                grads_ref[p],
                jnp.concatenate([acts, acts], axis=0),
                (((1,), (1,)), ((), ())),
                preferred_element_type=F32,
            )
    low = lax.broadcasted_iota(jnp.int32, (ROWS, 128), 1) < WIDTH
    for c in range(FEATURES // 128):
        even = wide_ref[pl.ds(2 * c, ROWS, stride=PITCH), :]
        odd = wide_ref[pl.ds(2 * c + 1, ROWS, stride=PITCH), :]
        out_ref[:, c * 128 : (c + 1) * 128] = jnp.where(low, even, odd).astype(BF16)


def query_grads(lengths, activations, out_grads, chunk):
    hbm = pl.BlockSpec(memory_space=pltpu.HBM)
    return pl.pallas_call(
        functools.partial(grad_kernel, chunk * ROWS),
        out_shape=jax.ShapeDtypeStruct((ROWS, FEATURES), BF16),
        in_specs=[hbm] * 3,
        scratch_shapes=[
            pltpu.VMEM((ROWS, WIDTH, SLOTS), BF16),
            pltpu.VMEM((ROWS, WIDTH, SLOTS), BF16),
            pltpu.SMEM((PAIRS,), jnp.int32),
            pltpu.VMEM((ROWS * PITCH, 128), F32),
            pltpu.SemaphoreType.DMA((2 * (ROWS // STEP_PAIRS) + 1,)),
        ],
        compiler_params=pltpu.CompilerParams(vmem_limit_bytes=16 << 20),
        name="query_grads",
    )(lengths, activations, out_grads)


def score_kernel(*refs):
    blocks, (mine_ref, other_ref), outs = refs[:8], refs[8:10], refs[10:14]
    rows_ref, sem = refs[14:]
    step = pl.program_id(0)
    x, _, y, z_hi, core = place()

    @pl.when(step == 0)
    def _():
        copies = [
            pltpu.make_async_copy(block, rows_ref.at[pl.ds(i * ROWS, ROWS)], sem.at[i])
            for i, block in enumerate(blocks)
        ]
        for copy in copies:
            copy.start()
        for copy in copies:
            copy.wait()

    def part(weights_ref, rel_core, tile):
        got = lax.dot_general(
            rows_ref[...],
            weights_ref[...],
            (((1,), (1,)), ((), ())),
            preferred_element_type=F32,
        ).astype(BF16)
        for rel_z in range(2):
            to_x = 2 * ((z_hi + rel_z) % 2) + core
            away = (to_x - x + 4) % 4
            if rel_core == 0:
                buf = jnp.where(away == 0, 1, jnp.where(away == 1, 3, jnp.where(away == 2, 2, 0)))
            else:
                buf = jnp.where(away == 0, 0, jnp.where(away == 1, 2, jnp.where(away == 2, 3, 1)))
            for b in range(4):

                @pl.when(buf == b)
                def _():
                    for j, dy in enumerate((0, 3, 1, 2)):
                        row = pl.multiple_of(((y + dy) % 4) * ROWS, ROWS)
                        at = (rel_z * 4 + j) * ROWS
                        outs[b][pl.ds(row, ROWS), tile * COLS : (tile + 1) * COLS] = got[at : at + ROWS]

    tiles = HELD // COLS
    for s in range(2 * tiles):

        @pl.when(step == s)
        def _():
            part(mine_ref if s < tiles else other_ref, s // tiles, s % tiles)


def partial_scores(blocks, mine, other):
    tiles = HELD // COLS
    out = pl.BlockSpec((4 * ROWS, HELD), lambda i: (0, 0))
    return pl.pallas_call(
        score_kernel,
        out_shape=[jax.ShapeDtypeStruct((4 * ROWS, HELD), BF16)] * 4,
        grid=(2 * tiles,),
        in_specs=[pl.BlockSpec(memory_space=pl.ANY)] * 8
        + [
            pl.BlockSpec((COLS, FEATURES), lambda i: (jnp.minimum(i, tiles - 1), 0)),
            pl.BlockSpec((COLS, FEATURES), lambda i: (jnp.maximum(i - tiles, 0), 0)),
        ],
        out_specs=[out] * 4,
        scratch_shapes=[
            pltpu.VMEM((8 * ROWS, FEATURES), BF16),
            pltpu.SemaphoreType.DMA((8,)),
        ],
        compiler_params=pltpu.CompilerParams(vmem_limit_bytes=18 << 20),
        cost_estimate=pl.CostEstimate(flops=1, bytes_accessed=1, transcendentals=0),
        name="partial_scores",
    )(*blocks, mine, other)


def cross_sum_kernel(b_ref, c_ref, a_ref, d_ref, own_ref, keep_ref, *outs):
    x, z_lo, _, _, core = place()
    match = (x % 2) == core
    for k in range(4):
        rows = pl.ds(pl.multiple_of(((z_lo + k) % 4) * ROWS, ROWS), ROWS)
        near = own_ref[rows, :].astype(F32) + b_ref[rows, :].astype(F32)
        last = jnp.where(match, near, d_ref[rows, :].astype(F32))
        total = (a_ref[rows, :].astype(F32) + c_ref[rows, :].astype(F32)) + last
        if k == 0:
            keep_ref[...] = total
        else:
            outs[k - 1][...] = total.astype(BF16)


def cross_sum(*parts):
    return pl.pallas_call(
        cross_sum_kernel,
        out_shape=[jax.ShapeDtypeStruct((ROWS, HELD), F32)]
        + [jax.ShapeDtypeStruct((ROWS, HELD), BF16)] * 3,
        compiler_params=pltpu.CompilerParams(vmem_limit_bytes=16 << 20),
        name="cross_sum",
    )(*parts)


def final_kernel(*refs):
    pick_ref, out_ref = refs[-2:]
    totals = []
    for n in range(CHUNKS):
        keep, first, second, third = refs[4 * n : 4 * n + 4]
        total = keep[...] + first[...].astype(F32)
        totals.append(total + (second[...].astype(F32) + third[...].astype(F32)))
    total = jnp.concatenate(totals, axis=0)
    high = total.astype(BF16)
    rest = total - high.astype(F32)
    middle = rest.astype(BF16)
    low = (rest - middle.astype(F32)).astype(BF16)
    picked = lax.dot_general(
        jnp.concatenate([high, middle, low], axis=0),
        pick_ref[...],
        (((1,), (0,)), ((), ())),
        preferred_element_type=F32,
    )
    out_ref[...] = picked[:PAIRS] + (picked[PAIRS : 2 * PAIRS] + picked[2 * PAIRS :])


def final_sum(parts, pick):
    return pl.pallas_call(
        final_kernel,
        out_shape=jax.ShapeDtypeStruct((PAIRS, HELD), F32),
        compiler_params=pltpu.CompilerParams(vmem_limit_bytes=16 << 20),
        name="final_sum",
    )(*parts, pick)


def store_pairs(move):
    pairs = []
    for z_lo in range(4):
        for x in range(4):
            pairs.append((node(x, z_lo, 0, 0, 0)[0], node(*move(x, z_lo), 0, 0, 0)[0]))
    return pairs


def all_pairs(move):
    pairs = []
    for z_lo in range(4):
        for x in range(4):
            for y in range(4):
                for z_hi in range(2):
                    for core in range(2):
                        dst = move(x, core)
                        if dst is None:
                            continue
                        s, g = node(x, z_lo, y, z_hi, core)
                        t, h = node(dst[0], z_lo, y, z_hi, dst[1])
                        pairs.append((s * 16 + g, t * 16 + h))
    return pairs


def along(value, move):
    return lax.ppermute(value, "group", group_pairs(move))


def fence_kernel(*refs):
    pass


def after(values, *others):
    hold = pl.BlockSpec(memory_space=pl.ANY)
    return pl.pallas_call(
        fence_kernel,
        out_shape=[jax.ShapeDtypeStruct(v.shape, v.dtype) for v in values],
        in_specs=[hold] * (len(values) + len(others)),
        out_specs=[hold] * len(values),
        input_output_aliases={i: i for i in range(len(values))},
        compiler_params=pltpu.CompilerParams(vmem_limit_bytes=1 << 20),
        name="fence",
    )(*values, *others)


def up(value):
    return along(value, lambda y, z, c: (y + 1, z, c))


def down(value):
    return along(value, lambda y, z, c: (y - 1, z, c))


def beyond(value):
    return along(value, lambda y, z, c: (y, z + 1, c))


def first_scores(a, b, stored, other):
    far_a = beyond(a)
    a_below, a_above = up(a), down(a)
    (b,) = after((b,), other)
    far_b = beyond(b)
    b_below, b_above = up(b), down(b)
    far_a, a_below, a_above = after((far_a, a_below, a_above), b_below, b_above)
    a_opposite = up(a_below)
    far_a_above, far_a_below = down(far_a), up(far_a)
    far_a_opposite = down(far_a_above)
    far_b, b_below = after((far_b, b_below), far_a_above, a_opposite)
    b_opposite = up(b_below)
    far_b_above, far_b_below = down(far_b), up(far_b)
    a_blocks = [a, a_below, a_above, a_opposite, far_a, far_a_below, far_a_above, far_a_opposite]
    a_bufs = list(partial_scores(a_blocks, stored, other))
    (far_b_above,) = after((far_b_above,), a_bufs[1])
    far_b_opposite = down(far_b_above)
    b_blocks = [b, b_below, b_above, b_opposite, far_b, far_b_below, far_b_above, far_b_opposite]
    return a_bufs, b_blocks


def join_kernel(send_ref, got_ref, out_ref):
    x, _, _, _, core = place()
    got = jnp.where((x % 2) == core, 0.0, got_ref[...].astype(F32))
    out_ref[...] = (send_ref[...].astype(F32) + got).astype(BF16)


def join(send, got):
    return pl.pallas_call(
        join_kernel,
        out_shape=jax.ShapeDtypeStruct(send.shape, BF16),
        compiler_params=pltpu.CompilerParams(vmem_limit_bytes=16 << 20),
        name="join",
    )(send, got)


def over_x(bufs):
    def send(value, move):
        return lax.ppermute(value, ("store", "group"), all_pairs(move))

    def match(x, core):
        return x % 2 == core

    got_b = send(bufs[3], lambda x, c: (x - 1, c) if match(x, c) else (x + 1, c))
    got_c = send(bufs[0], lambda x, c: (x, 1 - c) if match(x, c) else (x - 1, c))
    got_a = send(bufs[2], lambda x, c: (x + 2, c) if match(x, c) else (x + 1, 1 - c))
    joined = join(bufs[1], got_b)
    got_d = send(joined, lambda x, c: None if match(x, c) else (x - 1, 1 - c))
    return [got_b, got_c, got_a, got_d]


def on_device(activations, out_grads, stored, lengths, store_ids):
    stored = stored.reshape(HELD, FEATURES)
    other = lax.ppermute(stored, "group", group_pairs(lambda y, z, c: (y, z, 1 - c)))
    pick = (store_ids[None, :] == jnp.arange(HELD, dtype=jnp.int32)[:, None]).astype(BF16)
    inputs = [
        pltpu.with_memory_space_constraint(v, pltpu.HBM) for v in (lengths, activations, out_grads)
    ]
    a, b = (query_grads(*inputs, n) for n in range(CHUNKS))
    a_bufs, b_blocks = first_scores(a, b, stored, other)
    a_got = over_x(a_bufs)
    b_bufs = list(partial_scores(b_blocks, stored, other))
    b_bufs = after(b_bufs, *a_got[:3])
    b_got = over_x(b_bufs)
    parts = []
    for got, bufs in ((a_got, a_bufs), (b_got, b_bufs)):
        keep, *sends = cross_sum(*got, bufs[1])
        parts.append(keep)
        for k, send in enumerate(sends, 1):
            parts.append(lax.ppermute(send, "store", store_pairs(lambda x, z: (x, z + k))))
    return final_sum(parts, pick)


def solution(mesh):
    in_specs = (
        P("group", "store", None, None),
        P("group", "store", None, None),
        P("group", "store", None),
        P("group"),
        P("group"),
    )
    out_specs = P("store", "group")
    return jax.shard_map(
        on_device, mesh=mesh, in_specs=in_specs, out_specs=out_specs, check_vma=False
    )
```
